32 devices in a mesh: groups: 2 (over y), ep: 8 (over z, x), dp: 2 (over core).
Axes of the slice: x: 2, y: 2, z: 4, core: 2. Of those that a mesh axis runs over, the one named last changes fastest.
Arguments:
- tokens: bfloat16 [2048, 2048], P(('groups', 'ep'), 'dp'), parts along dimension 0, may hold values from -6 to 6
- out_grad: bfloat16 [2048, 2048], P(('groups', 'ep'), 'dp'), parts along dimension 0, may hold values from -6 to 6
- route_gates: bfloat16 [2048, 8], P(('groups', 'ep', 'dp')), parts along dimension 0, may hold values from 0.099609375 to 1
- expert_ids: int32 [2048, 8], P(('groups', 'ep', 'dp')), parts along dimension 0, may hold values from 0 to 127, all different within a row; in each aligned block of 64 rows (0 to 63, 64 to 127, ...) at most 6 rows name the same one
- w_gate: bfloat16 [128, 2048, 384], P('ep', 'dp'), may hold values from -0.125 to 0.125
- w_up: bfloat16 [128, 2048, 384], P('ep', 'dp'), may hold values from -0.125 to 0.125
- w_down: bfloat16 [128, 384, 2048], P('ep', None, 'dp'), may hold values from -0.3125 to 0.3125
Outputs:
- grad_input: bfloat16 [2048, 2048], P(('groups', 'ep'), 'dp'), parts along dimension 0
- grad_gate_w: bfloat16 [256, 2048, 384], P(('groups', 'ep'), 'dp'), parts along dimension 0
- grad_up_w: bfloat16 [256, 2048, 384], P(('groups', 'ep'), 'dp'), parts along dimension 0
The draws below stay inside these ranges and needn't reach their ends.
There are 2 independent parts, one for each index of `groups`. The reference program is written for one: setup_inputs(seed, part) draws one part's arguments, and reference() takes and returns one part's arrays. A program takes and returns all parts, laid end to end along the dimension named above; an argument that names none is the same for every part. Nothing has to cross between parts.
Inputs may be any that keep to these rules, and one draw needn't show every extreme that they name: `expert_ids`: each token names 8 different experts. In each aligned block of 64 tokens (the routing rows of one device) no expert is named by more than 6 tokens, and in every draw some block has an expert named by exactly 6.
All inputs are finite; a program needn't handle non-finite values.
Results may differ from the reference program's by a relative error of at most 0.0058.
Values may be sent and summed in bfloat16 or wider, within the bound.
No kernel may reach another device: no remote copies, remote signals or barrier semaphores. Data moves between devices by JAX's collectives and lax.ppermute only.
A program may use at most 320 MiB of HBM per device.

```python
import math
import jax
import jax.numpy as jnp
import numpy as np
from jax import lax

D = 2048
FF = 384
E = 128
TOP = 8
BLOCK = 64
CAP = 6
TOKENS = 1024


def levels(own_key, extent, pieces, low, largest):
    factor_of, own = 1.0, jax.random.fold_in(own_key, 6)
    for position, blocks in pieces:
        steps = jnp.exp(jax.random.uniform(jax.random.fold_in(own, position), (blocks,), jnp.float32, low / len(pieces), largest / len(pieces)))
        factor_of = factor_of * jnp.repeat(steps, extent[position] // blocks).reshape([-1 if axis == position else 1 for axis in range(len(extent))])
    return factor_of


def assign_block(rng, own, number, rows, count, top, reach, slope):
    order = jax.random.permutation(rng, count)
    crowded, usual = portions_of(count, rows * top, reach, slope, True), portions_of(count, rows * top, reach, slope, False)
    places = jnp.arange(count)

    def named(lengths, turn):
        used = int((lengths > 0).sum())
        fixed = max(1, used // 4)
        shifted = fixed + (places - fixed + turn * (used - fixed)) % max(1, count - fixed)
        return jnp.zeros((count,), jnp.int32).at[order[jnp.where(places < fixed, places, shifted)]].set(jnp.asarray(lengths, jnp.int32))

    lengths = jnp.where(number % 4 == 0, named(crowded, number // 4), named(usual, number - number // 4 - 1))
    mixed = jax.random.permutation(jax.random.fold_in(own, 3), count)
    source_of, receiver = mixed[0:count // 2 * 2:2], mixed[1:count // 2 * 2:2]
    margin = jnp.minimum(lengths[source_of] - 1, reach - lengths[receiver]) // 2
    margin = jnp.where((source_of == order[0]) | (receiver == order[0]) | (lengths[receiver] == 0), 0, jnp.maximum(margin, 0))
    shifted = jax.random.randint(jax.random.fold_in(own, 4), (count // 2,), 0, 1 << 20) % (margin + 1)
    lengths = lengths.at[source_of].add(-shifted).at[receiver].add(shifted)
    members = jnp.searchsorted(jnp.cumsum(lengths), jnp.arange(rows * top), side="right").astype(jnp.int32)
    table = members.reshape(top, rows).T
    table = table[jax.random.permutation(jax.random.fold_in(own, 1), rows)]
    turn = jax.random.randint(jax.random.fold_in(own, 2), (rows, 1), 0, top)
    return jnp.take_along_axis(table, (jnp.arange(top)[None, :] + turn) % top, axis=1)


def portions_of(amount, total, most, skew, full):
    weights = [(1 << 20) // math.isqrt(grade ** skew) + 1 for grade in range(1, amount + 1)]
    largest = most if full else min(most, max(-(-total // amount), total * weights[0] // sum(weights)))
    least = 1 if total - largest >= amount - 1 else 0
    counts, surplus = [largest] + [least] * (amount - 1), total - largest - least * (amount - 1)
    while surplus > 0:
        free = [i for i in range(1, amount) if counts[i] < largest] or [i for i in range(1, amount) if counts[i] < most]
        whole, remaining = sum([weights[i] for i in free]), surplus
        for i in free:
            more = min(most - counts[i], max(1, remaining * weights[i] // whole), surplus)
            counts[i] = counts[i] + more
            surplus = surplus - more
    return np.array(counts)


def scatter_about(stream_key, shape, scale, most, cuts=(), kind=jnp.bfloat16):
    drawn = scale * jax.random.normal(stream_key, shape, jnp.float32)
    if cuts:
        drawn = drawn * levels(stream_key, shape, cuts, -0.22, 0.18)
    return jnp.clip(drawn, -most, most).astype(kind)


def setup_inputs(seed: int = 0, part: int = 0) -> dict:
    key_of = jax.random.split(jax.random.key(seed), 8)
    part_splits = jax.random.split(jax.random.fold_in(key_of[7], part), 8)
    tokens = scatter_about(part_splits[0], (TOKENS, D), 1.0, 6.0, ((0, 8), (1, 2)))
    out_grad = scatter_about(part_splits[1], (TOKENS, D), 1.0, 6.0, ((0, 8), (1, 2)))
    route_gates = jnp.clip(0.099609375 + 0.9003906 * jax.random.uniform(part_splits[2], (TOKENS, TOP), jnp.float32) ** levels(part_splits[2], (TOKENS, TOP), ((0, 16),), -0.2, 0.2), 0.099609375, 1.0).astype(jnp.bfloat16)
    expert_ids_keys = jax.random.split(jax.random.fold_in(part_splits[3], 1), TOKENS // BLOCK)
    expert_ids_turns = jax.random.permutation(jax.random.fold_in(part_splits[3], 3), TOKENS // BLOCK)
    expert_ids = jax.vmap(lambda own, number: assign_block(jax.random.fold_in(part_splits[3], 2), own, number, BLOCK, E, TOP, CAP, 2))(expert_ids_keys, expert_ids_turns).reshape((TOKENS, TOP))
    w_gate = scatter_about(key_of[4], (E, D, FF), D ** -0.5, 0.125, ((0, 8), (1, 2)))
    w_up = scatter_about(key_of[5], (E, D, FF), D ** -0.5, 0.125, ((0, 8), (1, 2)))
    w_down = scatter_about(key_of[6], (E, FF, D), FF ** -0.5, 0.3125, ((0, 8), (2, 2)))
    return {"tokens": tokens, "out_grad": out_grad, "route_gates": route_gates, "expert_ids": expert_ids, "w_gate": w_gate, "w_up": w_up, "w_down": w_down}


def expert_pass(token_rows, grad_rows, gate_rows, gate_matrix, up_matrix, down_matrix):
    pre_gate = jnp.dot(token_rows, gate_matrix, preferred_element_type=jnp.float32)
    pre_up = jnp.dot(token_rows, up_matrix, preferred_element_type=jnp.float32)
    raw_down = jnp.dot(grad_rows, down_matrix.T, preferred_element_type=jnp.float32)
    grad_hidden = gate_rows.astype(jnp.float32)[:, None] * raw_down
    sigmoid = jax.nn.sigmoid(pre_gate)
    grad_gate_pre = (grad_hidden * pre_up * sigmoid * (1.0 + pre_gate * (1.0 - sigmoid))).astype(jnp.bfloat16)
    grad_up_pre = (grad_hidden * pre_gate * sigmoid).astype(jnp.bfloat16)
    row_grad = (jnp.dot(grad_gate_pre, gate_matrix.T, preferred_element_type=jnp.float32)
                + jnp.dot(grad_up_pre, up_matrix.T, preferred_element_type=jnp.float32)).astype(jnp.bfloat16)
    summed_gate = jnp.dot(token_rows.T, grad_gate_pre, preferred_element_type=jnp.float32)
    summed_up = jnp.dot(token_rows.T, grad_up_pre, preferred_element_type=jnp.float32)
    return row_grad, summed_gate.astype(jnp.bfloat16), summed_up.astype(jnp.bfloat16)


def reference(tokens, out_grad, route_gates, expert_ids, w_gate, w_up, w_down):
    blocks = TOKENS // BLOCK
    per_block = BLOCK * TOP
    slot_depth = blocks * CAP
    id_blocks = expert_ids.reshape(blocks, per_block)
    onehot = (id_blocks[:, :, None] == jnp.arange(E, dtype=jnp.int32)[None, None, :]).astype(jnp.int32)
    ranking = jnp.sum(onehot * (jnp.cumsum(onehot, axis=1) - 1), axis=2).astype(jnp.int32)
    block_number = jnp.arange(blocks, dtype=jnp.int32)[:, None]
    slot_ids = (id_blocks * slot_depth + block_number * CAP + ranking).reshape(-1).astype(jnp.int32)
    route_numbers = jnp.arange(TOKENS * TOP, dtype=jnp.int32)
    slot_table = jnp.full((E * slot_depth,), -1, jnp.int32).at[slot_ids].set(route_numbers)
    slot_table = slot_table.reshape(E, slot_depth)
    flat_gates = route_gates.reshape(-1)

    def expert_step(running, inputs):
        entries, gate_matrix, up_matrix, down_matrix = inputs
        occupied = entries >= 0
        route_id = jnp.maximum(entries, 0).astype(jnp.int32)
        token_id = (route_id // TOP).astype(jnp.int32)
        token_rows = tokens[token_id]
        grad_rows = out_grad[token_id]
        gate_rows = jnp.where(occupied, flat_gates[route_id], jnp.zeros_like(flat_gates[route_id]))
        row_grad, grad_gate, grad_up = expert_pass(token_rows, grad_rows, gate_rows,
                                                   gate_matrix, up_matrix, down_matrix)
        running = running.at[token_id].add(row_grad.astype(jnp.float32))
        return running, (grad_gate, grad_up)

    initial = jnp.zeros((TOKENS, D), jnp.float32)
    summed, (grad_gate_w, grad_up_w) = lax.scan(expert_step, initial, (slot_table, w_gate, w_up, w_down))
    return summed.astype(jnp.bfloat16), grad_gate_w, grad_up_w
```

```python
import functools

import jax
import jax.numpy as jnp
from jax import lax
from jax.experimental import pallas as pl
from jax.experimental.pallas import tpu as pltpu
from jax.sharding import PartitionSpec as P

CAP = 6
VMEM_LIMIT = 48 * 1024 * 1024


def route_slots(expert_ids, experts, stride, offset):
    flattened = expert_ids.reshape(-1)
    onehot = (flattened[:, None] == jnp.arange(experts, dtype=jnp.int32)[None, :]).astype(jnp.int32)
    ranking = jnp.sum(onehot * (jnp.cumsum(onehot, axis=0) - 1), axis=1)
    return flattened * stride + offset + ranking


def fill_slots(values, slot_ids, slot_count):
    zeroed = jnp.zeros((slot_count,) + values.shape[1:], values.dtype)
    return zeroed.at[slot_ids].set(values)


def swiglu_back(pre_gate, pre_up, raw_down, gate_rows):
    grad_hidden = gate_rows.astype(jnp.float32)[..., None] * raw_down
    sigmoid = jax.nn.sigmoid(pre_gate)
    grad_gate_pre = (grad_hidden * pre_up * sigmoid * (1.0 + pre_gate * (1.0 - sigmoid))).astype(
        jnp.bfloat16
    )
    grad_up_pre = (grad_hidden * pre_gate * sigmoid).astype(jnp.bfloat16)
    return (grad_gate_pre, grad_up_pre)


def share_pre_grads(grad_gate_pre, grad_up_pre):
    return (
        lax.all_gather(grad_gate_pre, "dp", axis=2, tiled=True),
        lax.all_gather(grad_up_pre, "dp", axis=2, tiled=True),
    )


def weight_terms(shaped_rows, both_gate, both_up):
    grad_gate_w = jnp.einsum(
        "nlbcd,nlbcf->ldf", shaped_rows, both_gate, preferred_element_type=jnp.float32
    )
    grad_up_w = jnp.einsum(
        "nlbcd,nlbcf->ldf", shaped_rows, both_up, preferred_element_type=jnp.float32
    )
    return (grad_gate_w.astype(jnp.bfloat16), grad_up_w.astype(jnp.bfloat16))


def expert_work(token_rows, grad_rows, gate_rows, w_gate, w_up, w_down):
    full_gate, full_up, full_down = (
        lax.all_gather(w_gate, "dp", axis=1, tiled=True),
        lax.all_gather(w_up, "dp", axis=1, tiled=True),
        lax.all_gather(w_down, "dp", axis=2, tiled=True),
    )
    pre_gate = jnp.einsum(
        "nlcd,ldf->nlcf", token_rows, full_gate, preferred_element_type=jnp.float32
    )
    pre_up = jnp.einsum("nlcd,ldf->nlcf", token_rows, full_up, preferred_element_type=jnp.float32)
    raw_down = jnp.einsum(
        "nlcd,lfd->nlcf", grad_rows, full_down, preferred_element_type=jnp.float32
    )
    grad_gate_pre, grad_up_pre = swiglu_back(pre_gate, pre_up, raw_down, gate_rows)
    row_grad = (
        jnp.einsum("nlcf,ldf->nlcd", grad_gate_pre, full_gate, preferred_element_type=jnp.float32)
        + jnp.einsum("nlcf,ldf->nlcd", grad_up_pre, full_up, preferred_element_type=jnp.float32)
    ).astype(jnp.bfloat16)
    return (row_grad, grad_gate_pre, grad_up_pre)


def exchange_body(tokens, out_grad, route_gates, expert_ids, w_gate, w_up, w_down):
    ep_count = lax.axis_size("ep")
    local_count = w_gate.shape[0]
    experts = local_count * ep_count
    block_rows, top_count = expert_ids.shape
    capacity = CAP
    half_width = tokens.shape[1]
    feature_width = 2 * half_width
    pair_ids = lax.all_gather(expert_ids, "dp", axis=0, tiled=True)
    first_slots = route_slots(pair_ids[:block_rows], experts, 2 * capacity, 0)
    second_slots = route_slots(pair_ids[block_rows:], experts, 2 * capacity, capacity)
    slot_ids = jnp.concatenate([first_slots, second_slots])
    own_slots = lax.dynamic_index_in_dim(
        slot_ids.reshape(2, block_rows * top_count), lax.axis_index("dp"), 0, keepdims=False
    )
    token_of = jnp.arange(2 * block_rows * top_count, dtype=jnp.int32) // top_count
    slot_count = experts * 2 * capacity
    send_rows = fill_slots(tokens[token_of], slot_ids, slot_count).reshape(
        ep_count, local_count * 2 * capacity, half_width
    )
    send_grads = fill_slots(out_grad[token_of], slot_ids, slot_count).reshape(
        ep_count, local_count * 2 * capacity, half_width
    )
    send_gates = fill_slots(route_gates.reshape(-1), own_slots, slot_count).reshape(
        ep_count, local_count * 2 * capacity
    )
    recv_rows, recv_grads, recv_gates = (
        lax.all_to_all(send_rows, "ep", split_axis=0, concat_axis=0, tiled=True),
        lax.all_to_all(send_grads, "ep", split_axis=0, concat_axis=0, tiled=True),
        lax.all_to_all(send_gates, "ep", split_axis=0, concat_axis=0, tiled=True),
    )
    shaped_rows = recv_rows.reshape(ep_count, local_count, 2, capacity, half_width)
    shaped_grads = recv_grads.reshape(ep_count, local_count, 2, capacity, half_width)
    shaped_gates = recv_gates.reshape(ep_count, local_count, 2, capacity)
    joined_rows, joined_grads = (
        lax.all_to_all(shaped_rows, "dp", split_axis=2, concat_axis=4, tiled=True),
        lax.all_to_all(shaped_grads, "dp", split_axis=2, concat_axis=4, tiled=True),
    )
    token_rows = joined_rows.reshape(ep_count, local_count, capacity, feature_width)
    grad_rows = joined_grads.reshape(ep_count, local_count, capacity, feature_width)
    gate_rows = lax.dynamic_index_in_dim(shaped_gates, lax.axis_index("dp"), 2, keepdims=False)
    row_grad, grad_gate_pre, grad_up_pre = expert_work(
        token_rows, grad_rows, gate_rows, w_gate, w_up, w_down
    )
    both_gate, both_up = share_pre_grads(
        grad_gate_pre.reshape(ep_count, local_count, 1, capacity, -1),
        grad_up_pre.reshape(ep_count, local_count, 1, capacity, -1),
    )
    spread = lax.all_to_all(
        row_grad.reshape(ep_count, local_count, 1, capacity, feature_width),
        "dp",
        split_axis=4,
        concat_axis=2,
        tiled=True,
    )
    grad_gate_w, grad_up_w = weight_terms(shaped_rows, both_gate, both_up)
    returned = lax.all_to_all(
        spread.reshape(ep_count, local_count * 2 * capacity, half_width),
        "ep",
        split_axis=0,
        concat_axis=0,
        tiled=True,
    )
    returned = returned.reshape(slot_count, half_width)
    per_route = (
        returned[slot_ids].astype(jnp.float32).reshape(2 * block_rows, top_count, half_width)
    )
    grad_input = jnp.sum(per_route, axis=1).astype(jnp.bfloat16)
    return (grad_input, grad_gate_w, grad_up_w)


def arrival_orders(lines):
    orders = []
    for here in range(lines):
        flip = here >= (lines + 1) // 2
        near = sorted(
            (j for j in range(lines) if j != here),
            key=lambda j: (abs(j - here), (j < here) if flip else (j > here)),
        )
        orders.append([here] + near)
    return orders


def pick(here, choices):
    result, distinct = choices[0], []
    for position, value in enumerate(choices):
        if not any(value is seen for seen, _ in distinct):
            distinct.append((value, [position]))
        else:
            for seen, places in distinct:
                if seen is value:
                    places.append(position)
    result = distinct[0][0]
    for value, places in distinct[1:]:
        chosen = functools.reduce(jnp.logical_or, [here == place for place in places])
        result = jnp.where(chosen, value, result)
    return result


def along_line(value, lines, upward, first):
    if upward:
        moves = [(q, q + 1) for q in range(lines - 1) if q >= first]
    else:
        moves = [(q, q - 1) for q in range(1, lines) if lines - 1 - q >= first]
    pairs = [(2 * a + side, 2 * b + side) for a, b in moves for side in range(2)]
    return lax.ppermute(value, "ep", pairs)


def across_pair(value, lines):
    return lax.ppermute(value, "ep", [(i, i ^ 1) for i in range(2 * lines)])


def across_cores(value):
    return lax.ppermute(value, "dp", [(0, 1), (1, 0)])


def gather_pieces(value, lines, here, orders):
    ups, downs = [], []
    up = down = value
    for step in range(lines - 1):
        up, down = along_line(up, lines, True, step), along_line(down, lines, False, step)
        ups.append(up)
        downs.append(down)
    pieces = []
    for m in range(lines):
        choices = []
        for q in range(lines):
            source = orders[q][m]
            if source == q:
                choices.append(value)
            elif source < q:
                choices.append(ups[q - source - 1])
            else:
                choices.append(downs[source - q - 1])
        own = pick(here, choices)
        pieces += [own, across_pair(own, lines)]
    return pieces


def scatter_sums(partial, lines, here, orders):
    halves = [None] * lines
    for m in reversed(range(lines)):
        other = across_pair(partial[2 * m + 1], lines)
        halves[m] = partial[2 * m].astype(jnp.float32) + other.astype(jnp.float32)
    up = down = None
    for step in range(1, lines):
        reach = lines - step
        moved = []
        for upward, came in ((True, up), (False, down)):
            choices = []
            for q in range(lines):
                target = q + reach if upward else q - reach
                usable = 0 <= target < lines
                choices.append(halves[orders[q].index(target)] if usable else None)
            spare = next(c for c in choices if c is not None)
            total = pick(here, [spare if c is None else c for c in choices])
            if came is not None:
                total = total + came.astype(jnp.float32)
            total = total.astype(jnp.bfloat16)
            if upward:
                moves = [(q, q + 1) for q in range(lines) if q + reach < lines]
            else:
                moves = [(q, q - 1) for q in range(lines) if q - reach >= 0]
            pairs = [(2 * a + side, 2 * b + side) for a, b in moves for side in range(2)]
            moved.append(lax.ppermute(total, "ep", pairs))
        up, down = moved
    total = halves[0]
    if lines > 1:
        total = total + up.astype(jnp.float32) + down.astype(jnp.float32)
    return total.astype(jnp.bfloat16)


def route_kernel(order_ref, base_ref, info_ref, slot_ref, gate_ref, *, top_count, block_rows):
    local_count = slot_ref.shape[0]
    chunk = info_ref.shape[2]
    row = lax.broadcasted_iota(jnp.int32, (chunk, chunk), 0)
    column = lax.broadcasted_iota(jnp.int32, (chunk, chunk), 1)
    before = ((row < column) & (row // block_rows == column // block_rows)).astype(jnp.bfloat16)
    lane = lax.broadcasted_iota(jnp.int32, (local_count, chunk), 1)
    expert = (base_ref[0] + lax.broadcasted_iota(jnp.int32, (local_count, chunk), 0)).astype(
        jnp.float32
    )
    for piece in range(info_ref.shape[0]):
        info = info_ref[order_ref[piece]].astype(jnp.float32)
        named = jnp.zeros((local_count, chunk), jnp.float32)
        gate = jnp.zeros((local_count, chunk), jnp.float32)
        for k in range(top_count):
            match = info[k : k + 1, :] == expert
            named = jnp.where(match, 1.0, named)
            gate = jnp.where(match, info[top_count + k : top_count + k + 1, :], gate)
        rank = jnp.dot(
            named.astype(jnp.bfloat16), before, preferred_element_type=jnp.float32
        ).astype(jnp.int32)
        block = piece * (chunk // block_rows) + lane // block_rows
        columns = pl.ds(piece * chunk, chunk)
        slot_ref[:, columns] = jnp.where(named > 0.5, block * CAP + rank, -1)
        gate_ref[:, columns] = gate


def one_hot(slot_ref, expert, slots):
    tokens = slot_ref.shape[1]
    own = slot_ref[pl.ds(expert, 1), :]
    return lax.broadcasted_iota(jnp.int32, (slots, tokens), 0) == own


def collect_rows(piece_refs, rows_ref, sems):
    chunk = piece_refs[0].shape[0]
    copies = [
        pltpu.make_async_copy(ref, rows_ref.at[pl.ds(m * chunk, chunk)], sems.at[m])
        for m, ref in enumerate(piece_refs)
    ]
    for copy in copies:
        copy.start()
    for copy in copies:
        copy.wait()


def pre_kernel(count, slots, slot_ref, *refs):
    pieces = refs[:count]
    gate_w_ref, up_w_ref, x_ref, gate_ref, up_ref, rows_ref, sems = refs[count:]
    step = pl.program_id(0)
    batch = gate_w_ref.shape[0]

    @pl.when(step == 0)
    def _():
        collect_rows(pieces, rows_ref, sems)

    hot = jnp.concatenate(
        [one_hot(slot_ref, step * batch + i, slots).astype(jnp.bfloat16) for i in range(batch)]
    )
    x = jnp.dot(hot, rows_ref[...], preferred_element_type=jnp.float32).astype(jnp.bfloat16)
    for i in range(batch):
        own = x[i * slots : (i + 1) * slots]
        x_ref[i] = own
        gate_ref[i] = jnp.dot(own, gate_w_ref[i], preferred_element_type=jnp.float32)
        up_ref[i] = jnp.dot(own, up_w_ref[i], preferred_element_type=jnp.float32)


def down_kernel(count, slots, slot_ref, gates_ref, *refs):
    pieces = refs[:count]
    down_w_ref, raw_ref, rows_ref, sems = refs[count:]
    step = pl.program_id(0)
    batch = down_w_ref.shape[0]

    @pl.when(step == 0)
    def _():
        collect_rows(pieces, rows_ref, sems)

    hots = [one_hot(slot_ref, step * batch + i, slots) for i in range(batch)]
    hot = jnp.concatenate([h.astype(jnp.bfloat16) for h in hots])
    x = jnp.dot(hot, rows_ref[...], preferred_element_type=jnp.float32).astype(jnp.bfloat16)
    for i in range(batch):
        own = x[i * slots : (i + 1) * slots]
        raw = lax.dot_general(
            own, down_w_ref[i], (((1,), (1,)), ((), ())), preferred_element_type=jnp.float32
        )
        gates = gates_ref[pl.ds(step * batch + i, 1), :]
        gate = jnp.sum(jnp.where(hots[i], gates, 0.0), axis=1, keepdims=True)
        raw_ref[i] = gate * raw


def add_rows(slot_ref, step, slots, grads, gate_w_ref, up_w_ref, sum_ref, out_ref):
    batch = gate_w_ref.shape[0]
    contract = (((1,), (1,)), ((), ()))
    hots, rows = [], []
    for i, (grad_gate, grad_up) in enumerate(grads):
        row = lax.dot_general(
            grad_gate, gate_w_ref[i], contract, preferred_element_type=jnp.float32
        ) + lax.dot_general(grad_up, up_w_ref[i], contract, preferred_element_type=jnp.float32)
        rows.append(row.astype(jnp.bfloat16))
        hots.append(one_hot(slot_ref, step * batch + i, slots).astype(jnp.bfloat16))
    added = lax.dot_general(
        jnp.concatenate(hots),
        jnp.concatenate(rows),
        (((0,), (0,)), ((), ())),
        preferred_element_type=jnp.float32,
    )

    @pl.when(step == 0)
    def _():
        sum_ref[...] = added

    @pl.when(step > 0)
    def _():
        sum_ref[...] += added

    @pl.when(step == pl.num_programs(0) - 1)
    def _():
        out_ref[...] = sum_ref[...].astype(jnp.bfloat16)


def first_rows_kernel(
    slots,
    slot_ref,
    gate_own,
    gate_other,
    up_own,
    up_other,
    raw_own,
    raw_other,
    gate_w_ref,
    up_w_ref,
    grad_gate_ref,
    grad_up_ref,
    out_ref,
    sum_ref,
):
    step = pl.program_id(0)
    batch = gate_w_ref.shape[0]
    grads = []
    for i in range(batch):
        pre_gate = gate_own[i] + gate_other[i]
        pre_up = up_own[i] + up_other[i]
        grad_hidden = raw_own[i] + raw_other[i]
        sigmoid = jax.nn.sigmoid(pre_gate)
        scaled = grad_hidden * sigmoid
        grad_gate = (scaled * pre_up * (1.0 + pre_gate * (1.0 - sigmoid))).astype(jnp.bfloat16)
        grad_up = (scaled * pre_gate).astype(jnp.bfloat16)
        grad_gate_ref[i] = grad_gate
        grad_up_ref[i] = grad_up
        grads.append((grad_gate, grad_up))
    add_rows(slot_ref, step, slots, grads, gate_w_ref, up_w_ref, sum_ref, out_ref)


def later_rows_kernel(
    slots, slot_ref, grad_gate_ref, grad_up_ref, gate_w_ref, up_w_ref, out_ref, sum_ref
):
    grads = [(grad_gate_ref[i], grad_up_ref[i]) for i in range(gate_w_ref.shape[0])]
    add_rows(slot_ref, pl.program_id(0), slots, grads, gate_w_ref, up_w_ref, sum_ref, out_ref)


def weight_kernel(x_ref, grad_gate_ref, grad_up_ref, gate_out_ref, up_out_ref):
    contract = (((0,), (0,)), ((), ()))
    for i in range(x_ref.shape[0]):
        x = x_ref[i]
        gate_out_ref[i] = lax.dot_general(
            x, grad_gate_ref[i], contract, preferred_element_type=jnp.float32
        ).astype(jnp.bfloat16)
        up_out_ref[i] = lax.dot_general(
            x, grad_up_ref[i], contract, preferred_element_type=jnp.float32
        ).astype(jnp.bfloat16)


def params():
    return pltpu.CompilerParams(
        vmem_limit_bytes=VMEM_LIMIT, dimension_semantics=("arbitrary",)
    )


def cost(flops, moved):
    return pl.CostEstimate(flops=int(flops), bytes_accessed=int(moved), transcendentals=0)


def whole(*shape):
    return pl.BlockSpec(shape, lambda e: (0,) * len(shape))


def batched(batch, *shape):
    return pl.BlockSpec((batch,) + shape, lambda e: (e,) + (0,) * len(shape))


def gather_body(tokens, out_grad, route_gates, expert_ids, w_gate, w_up, w_down):
    ep_count = lax.axis_size("ep")
    lines = ep_count // 2
    local_count, half_width, hidden = w_gate.shape
    block_rows, top_count = expert_ids.shape
    chunk = 2 * block_rows
    token_count = ep_count * chunk
    slots = 2 * ep_count * CAP
    chunks = 2
    width = half_width // chunks
    batch = 2 if local_count % 2 == 0 else 1
    steps = local_count // batch
    place = lax.axis_index("ep")
    here, side = place // 2, place % 2
    orders = arrival_orders(lines)
    bf16, f32 = jnp.bfloat16, jnp.float32
    memory = pl.BlockSpec(memory_space=pl.ANY)
    smem = pl.BlockSpec(memory_space=pltpu.SMEM)
    vmem = pl.BlockSpec(memory_space=pltpu.VMEM)

    own_info = jnp.concatenate([expert_ids.astype(bf16), route_gates], axis=1).T
    info = jnp.zeros((ep_count, 2 * top_count, chunk), bf16)
    info = lax.dynamic_update_slice(
        info, own_info[None], (place, 0, lax.axis_index("dp") * block_rows)
    )
    info = info + across_cores(info)
    bit = 1
    while bit < ep_count:
        info = info + lax.ppermute(info, "ep", [(i, i ^ bit) for i in range(ep_count)])
        bit *= 2

    token_pieces = gather_pieces(tokens, lines, here, orders)
    grad_pieces = gather_pieces(out_grad, lines, here, orders)

    line_order = jnp.asarray(orders, jnp.int32)[here]
    order = (2 * line_order[:, None] + jnp.stack([side, 1 - side])[None, :]).reshape(-1)
    slot_of, gate_of = pl.pallas_call(
        functools.partial(route_kernel, top_count=top_count, block_rows=block_rows),
        out_shape=(
            jax.ShapeDtypeStruct((local_count, token_count), jnp.int32),
            jax.ShapeDtypeStruct((local_count, token_count), f32),
        ),
        in_specs=[smem, smem, vmem],
        out_specs=(vmem, vmem),
        compiler_params=pltpu.CompilerParams(vmem_limit_bytes=VMEM_LIMIT),
        cost_estimate=cost(1e7, 1e6),
        name="route",
    )(order, (place * local_count).reshape(1), info)

    rows_scratch = [
        pltpu.VMEM((token_count, half_width), bf16),
        pltpu.SemaphoreType.DMA((ep_count,)),
    ]
    weight_bytes = local_count * half_width * hidden * 2
    matmul_flops = 2 * local_count * slots * half_width * hidden
    hot_flops = 2 * local_count * slots * half_width * token_count
    pre_shape = jax.ShapeDtypeStruct((local_count, slots, hidden), f32)
    grad_shape = jax.ShapeDtypeStruct((local_count, slots, hidden), bf16)
    x, gate_part, up_part = pl.pallas_call(
        functools.partial(pre_kernel, ep_count, slots),
        grid=(steps,),
        out_shape=(
            jax.ShapeDtypeStruct((local_count, slots, half_width), bf16),
            pre_shape,
            pre_shape,
        ),
        in_specs=[whole(local_count, token_count)]
        + [memory] * ep_count
        + [batched(batch, half_width, hidden)] * 2,
        out_specs=(
            batched(batch, slots, half_width),
            batched(batch, slots, hidden),
            batched(batch, slots, hidden),
        ),
        scratch_shapes=rows_scratch,
        compiler_params=params(),
        cost_estimate=cost(hot_flops + 2 * matmul_flops, 2.5 * weight_bytes),
        name="pre",
    )(slot_of, *token_pieces, w_gate, w_up)
    gate_other, up_other = across_cores(gate_part), across_cores(up_part)

    raw_part = pl.pallas_call(
        functools.partial(down_kernel, ep_count, slots),
        grid=(steps,),
        out_shape=pre_shape,
        in_specs=[whole(local_count, token_count)] * 2
        + [memory] * ep_count
        + [batched(batch, hidden, half_width)],
        out_specs=batched(batch, slots, hidden),
        scratch_shapes=rows_scratch,
        compiler_params=params(),
        cost_estimate=cost(hot_flops + matmul_flops, 1.3 * weight_bytes),
        name="down",
    )(slot_of, gate_of, *grad_pieces, w_down)
    raw_other = across_cores(raw_part)

    def part_of_weights(number):
        return pl.BlockSpec((batch, width, hidden), lambda e: (e, number, 0))

    rows_cost = cost(
        (2 * matmul_flops + hot_flops) / chunks, 2 * weight_bytes / chunks + weight_bytes / 2
    )
    sums = jax.ShapeDtypeStruct((token_count, width), bf16)
    sum_scratch = [pltpu.VMEM((token_count, width), f32)]
    grad_gate, grad_up, partial = pl.pallas_call(
        functools.partial(first_rows_kernel, slots),
        grid=(steps,),
        out_shape=(grad_shape, grad_shape, sums),
        in_specs=[whole(local_count, token_count)]
        + [batched(batch, slots, hidden)] * 6
        + [part_of_weights(0)] * 2,
        out_specs=(
            batched(batch, slots, hidden),
            batched(batch, slots, hidden),
            whole(token_count, width),
        ),
        scratch_shapes=sum_scratch,
        compiler_params=params(),
        cost_estimate=rows_cost,
        name="rows_first",
    )(slot_of, gate_part, gate_other, up_part, up_other, raw_part, raw_other, w_gate, w_up)
    partials = [partial]
    for number in range(1, chunks):
        partials.append(
            pl.pallas_call(
                functools.partial(later_rows_kernel, slots),
                grid=(steps,),
                out_shape=sums,
                in_specs=[whole(local_count, token_count)]
                + [batched(batch, slots, hidden)] * 2
                + [part_of_weights(number)] * 2,
                out_specs=whole(token_count, width),
                scratch_shapes=sum_scratch,
                compiler_params=params(),
                cost_estimate=rows_cost,
                name="rows_later",
            )(slot_of, grad_gate, grad_up, w_gate, w_up)
        )
    weight_shape = jax.ShapeDtypeStruct(w_gate.shape, bf16)
    grad_gate_w, grad_up_w = pl.pallas_call(
        weight_kernel,
        grid=(steps,),
        out_shape=(weight_shape, weight_shape),
        in_specs=[batched(batch, slots, half_width)] + [batched(batch, slots, hidden)] * 2,
        out_specs=(batched(batch, half_width, hidden), batched(batch, half_width, hidden)),
        compiler_params=params(),
        cost_estimate=cost(2 * matmul_flops, 2.5 * weight_bytes),
        name="weight_grads",
    )(x, grad_gate, grad_up)

    returned = [
        scatter_sums(value.reshape(ep_count, chunk, width), lines, here, orders)
        for value in partials
    ]
    return (jnp.concatenate(returned, axis=1), grad_gate_w, grad_up_w)


def solution(mesh):
    in_specs = (
        P(("groups", "ep"), "dp"),
        P(("groups", "ep"), "dp"),
        P(("groups", "ep", "dp"), None),
        P(("groups", "ep", "dp"), None),
        P("ep", "dp", None),
        P("ep", "dp", None),
        P("ep", None, "dp"),
    )
    out_specs = (
        P(("groups", "ep"), "dp"),
        P(("groups", "ep"), "dp", None),
        P(("groups", "ep"), "dp", None),
    )
    ep_count = mesh.shape["ep"]
    body = gather_body if ep_count in (2, 4, 8) else exchange_body
    return jax.shard_map(body, mesh=mesh, in_specs=in_specs, out_specs=out_specs, check_vma=False)
```

```python
import functools

import jax
import jax.numpy as jnp
from jax import lax
from jax.experimental import pallas as pl
from jax.experimental.pallas import tpu as pltpu
from jax.sharding import PartitionSpec as P

CAP = 6


def route_slots(expert_ids, experts, stride, offset):
    flattened = expert_ids.reshape(-1)
    onehot = (flattened[:, None] == jnp.arange(experts, dtype=jnp.int32)[None, :]).astype(jnp.int32)
    ranking = jnp.sum(onehot * (jnp.cumsum(onehot, axis=0) - 1), axis=1)
    return flattened * stride + offset + ranking


def fill_slots(values, slot_ids, slot_count):
    zeroed = jnp.zeros((slot_count,) + values.shape[1:], values.dtype)
    return zeroed.at[slot_ids].set(values)


def swiglu_back(pre_gate, pre_up, raw_down, gate_rows):
    grad_hidden = gate_rows.astype(jnp.float32)[..., None] * raw_down
    sigmoid = jax.nn.sigmoid(pre_gate)
    grad_gate_pre = (grad_hidden * pre_up * sigmoid * (1.0 + pre_gate * (1.0 - sigmoid))).astype(
        jnp.bfloat16
    )
    grad_up_pre = (grad_hidden * pre_gate * sigmoid).astype(jnp.bfloat16)
    return (grad_gate_pre, grad_up_pre)


def share_pre_grads(grad_gate_pre, grad_up_pre):
    return (
        lax.all_gather(grad_gate_pre, "dp", axis=2, tiled=True),
        lax.all_gather(grad_up_pre, "dp", axis=2, tiled=True),
    )


def weight_terms(shaped_rows, both_gate, both_up):
    grad_gate_w = jnp.einsum(
        "nlbcd,nlbcf->ldf", shaped_rows, both_gate, preferred_element_type=jnp.float32
    )
    grad_up_w = jnp.einsum(
        "nlbcd,nlbcf->ldf", shaped_rows, both_up, preferred_element_type=jnp.float32
    )
    return (grad_gate_w.astype(jnp.bfloat16), grad_up_w.astype(jnp.bfloat16))


def expert_work(token_rows, grad_rows, gate_rows, w_gate, w_up, w_down):
    full_gate, full_up, full_down = (
        lax.all_gather(w_gate, "dp", axis=1, tiled=True),
        lax.all_gather(w_up, "dp", axis=1, tiled=True),
        lax.all_gather(w_down, "dp", axis=2, tiled=True),
    )
    pre_gate = jnp.einsum(
        "nlcd,ldf->nlcf", token_rows, full_gate, preferred_element_type=jnp.float32
    )
    pre_up = jnp.einsum("nlcd,ldf->nlcf", token_rows, full_up, preferred_element_type=jnp.float32)
    raw_down = jnp.einsum(
        "nlcd,lfd->nlcf", grad_rows, full_down, preferred_element_type=jnp.float32
    )
    grad_gate_pre, grad_up_pre = swiglu_back(pre_gate, pre_up, raw_down, gate_rows)
    row_grad = (
        jnp.einsum("nlcf,ldf->nlcd", grad_gate_pre, full_gate, preferred_element_type=jnp.float32)
        + jnp.einsum("nlcf,ldf->nlcd", grad_up_pre, full_up, preferred_element_type=jnp.float32)
    ).astype(jnp.bfloat16)
    return (row_grad, grad_gate_pre, grad_up_pre)


def exchange_body(tokens, out_grad, route_gates, expert_ids, w_gate, w_up, w_down):
    ep_count = lax.axis_size("ep")
    local_count = w_gate.shape[0]
    experts = local_count * ep_count
    block_rows, top_count = expert_ids.shape
    capacity = CAP
    half_width = tokens.shape[1]
    feature_width = 2 * half_width
    pair_ids = lax.all_gather(expert_ids, "dp", axis=0, tiled=True)
    first_slots = route_slots(pair_ids[:block_rows], experts, 2 * capacity, 0)
    second_slots = route_slots(pair_ids[block_rows:], experts, 2 * capacity, capacity)
    slot_ids = jnp.concatenate([first_slots, second_slots])
    own_slots = lax.dynamic_index_in_dim(
        slot_ids.reshape(2, block_rows * top_count), lax.axis_index("dp"), 0, keepdims=False
    )
    token_of = jnp.arange(2 * block_rows * top_count, dtype=jnp.int32) // top_count
    slot_count = experts * 2 * capacity
    send_rows = fill_slots(tokens[token_of], slot_ids, slot_count).reshape(
        ep_count, local_count * 2 * capacity, half_width
    )
    send_grads = fill_slots(out_grad[token_of], slot_ids, slot_count).reshape(
        ep_count, local_count * 2 * capacity, half_width
    )
    send_gates = fill_slots(route_gates.reshape(-1), own_slots, slot_count).reshape(
        ep_count, local_count * 2 * capacity
    )
    recv_rows, recv_grads, recv_gates = (
        lax.all_to_all(send_rows, "ep", split_axis=0, concat_axis=0, tiled=True),
        lax.all_to_all(send_grads, "ep", split_axis=0, concat_axis=0, tiled=True),
        lax.all_to_all(send_gates, "ep", split_axis=0, concat_axis=0, tiled=True),
    )
    shaped_rows = recv_rows.reshape(ep_count, local_count, 2, capacity, half_width)
    shaped_grads = recv_grads.reshape(ep_count, local_count, 2, capacity, half_width)
    shaped_gates = recv_gates.reshape(ep_count, local_count, 2, capacity)
    joined_rows, joined_grads = (
        lax.all_to_all(shaped_rows, "dp", split_axis=2, concat_axis=4, tiled=True),
        lax.all_to_all(shaped_grads, "dp", split_axis=2, concat_axis=4, tiled=True),
    )
    token_rows = joined_rows.reshape(ep_count, local_count, capacity, feature_width)
    grad_rows = joined_grads.reshape(ep_count, local_count, capacity, feature_width)
    gate_rows = lax.dynamic_index_in_dim(shaped_gates, lax.axis_index("dp"), 2, keepdims=False)
    row_grad, grad_gate_pre, grad_up_pre = expert_work(
        token_rows, grad_rows, gate_rows, w_gate, w_up, w_down
    )
    both_gate, both_up = share_pre_grads(
        grad_gate_pre.reshape(ep_count, local_count, 1, capacity, -1),
        grad_up_pre.reshape(ep_count, local_count, 1, capacity, -1),
    )
    spread = lax.all_to_all(
        row_grad.reshape(ep_count, local_count, 1, capacity, feature_width),
        "dp",
        split_axis=4,
        concat_axis=2,
        tiled=True,
    )
    grad_gate_w, grad_up_w = weight_terms(shaped_rows, both_gate, both_up)
    returned = lax.all_to_all(
        spread.reshape(ep_count, local_count * 2 * capacity, half_width),
        "ep",
        split_axis=0,
        concat_axis=0,
        tiled=True,
    )
    returned = returned.reshape(slot_count, half_width)
    per_route = (
        returned[slot_ids].astype(jnp.float32).reshape(2 * block_rows, top_count, half_width)
    )
    grad_input = jnp.sum(per_route, axis=1).astype(jnp.bfloat16)
    return (grad_input, grad_gate_w, grad_up_w)


ORDERS = ((0, 1, 2, 3), (1, 0, 2, 3), (2, 3, 1, 0), (3, 2, 1, 0))
LINES = len(ORDERS)
PARTS = 2
OUTER = ((0, 1), (1, 0), (2, 3), (3, 2))
INNER = ((1, 2), (2, 1))
TO_END = ((1, 0), (2, 3))
FROM_END = ((0, 1), (3, 2))


def along_line(value, moves):
    pairs = [(2 * a + side, 2 * b + side) for a, b in moves for side in range(2)]
    return lax.ppermute(value, "ep", pairs)


def across_pair(value):
    return lax.ppermute(value, "ep", [(i, i ^ 1) for i in range(2 * LINES)])


def across_cores(value):
    return lax.ppermute(value, "dp", [(0, 1), (1, 0)])


def tie(values, *others):
    values = list(values)
    return list(lax.optimization_barrier(tuple(values) + tuple(others))[: len(values)])


def gather_rows(rows, info, at_end, meanwhile):
    def widen(info, bits):
        came = [
            lax.ppermute(info, "ep", [(i, i ^ bit) for i in range(2 * LINES)]) for bit in bits
        ]
        return functools.reduce(jnp.add, came, info)

    outer, inner, other = along_line(rows, OUTER), along_line(rows, INNER), across_pair(rows)
    info = widen(info + across_cores(info), [1])
    outer, inner, other, info = tie((outer, inner, other, info))
    pieces = [rows, other]

    info = widen(info, [2, 4, 6])
    outer, inner, info = tie((outer, inner, info))
    second, third = along_line(inner, TO_END), along_line(outer, INNER)
    other = across_pair(outer)
    done = meanwhile(0, info, pieces)
    second, third, other = tie((second, third, other), *done)
    pieces += [outer, other]

    middle = jnp.where(at_end, second, inner)
    last, other = along_line(third, TO_END), across_pair(middle)
    done = meanwhile(1, info, pieces)
    last, other = tie((last, other), *done)
    pieces += [middle, other]

    meanwhile(2, info, [last, other])
    for part in range(2):
        far = jnp.where(at_end, last[part], third[part])
        pieces += [far, across_pair(far)]
        last, third = tie((last, third))
    return pieces


def scatter_sums(partial, meanwhile):
    f32, bf16 = jnp.float32, jnp.bfloat16

    def own_side(m, other):
        return partial[2 * m].astype(f32) + other.astype(f32)

    other = across_pair(partial[7])
    (other,) = meanwhile(0, [other])
    far = own_side(3, other)
    outward, other = along_line(far.astype(bf16), FROM_END), across_pair(partial[5])
    outward, other = meanwhile(1, [outward, other])
    middle = own_side(2, other)
    crossed = along_line((far + outward.astype(f32)).astype(bf16), INNER)
    outward, other = along_line(middle.astype(bf16), FROM_END), across_pair(partial[3])
    crossed, outward, other = meanwhile(2, [crossed, outward, other])
    near = own_side(1, other) + crossed.astype(f32)
    inner = along_line((middle + outward.astype(f32)).astype(bf16), INNER)
    outer, other = along_line(near.astype(bf16), OUTER), across_pair(partial[1])
    inner, outer, other = meanwhile(3, [inner, outer, other])
    total = own_side(0, other) + outer.astype(f32) + inner.astype(f32)
    return total.astype(bf16)


def route_kernel(order_ref, base_ref, info_ref, slot_ref, gate_ref, *, top_count, block_rows):
    local_count = slot_ref.shape[0]
    chunk = info_ref.shape[2]
    row = lax.broadcasted_iota(jnp.int32, (chunk, chunk), 0)
    column = lax.broadcasted_iota(jnp.int32, (chunk, chunk), 1)
    before = ((row < column) & (row // block_rows == column // block_rows)).astype(jnp.bfloat16)
    lane = lax.broadcasted_iota(jnp.int32, (local_count, chunk), 1)
    expert = (base_ref[0] + lax.broadcasted_iota(jnp.int32, (local_count, chunk), 0)).astype(
        jnp.float32
    )
    for piece in range(info_ref.shape[0]):
        info = info_ref[order_ref[piece]].astype(jnp.float32)
        named = jnp.zeros((local_count, chunk), jnp.float32)
        gate = jnp.zeros((local_count, chunk), jnp.float32)
        for k in range(top_count):
            match = info[k : k + 1, :] == expert
            named = jnp.where(match, 1.0, named)
            gate = jnp.where(match, info[top_count + k : top_count + k + 1, :], gate)
        rank = jnp.dot(
            named.astype(jnp.bfloat16), before, preferred_element_type=jnp.float32
        ).astype(jnp.int32)
        block = piece * (chunk // block_rows) + lane // block_rows
        columns = pl.ds(piece * chunk, chunk)
        slot_ref[:, columns] = jnp.where(named > 0.5, block * CAP + rank, -1)
        gate_ref[:, columns] = gate


def start_all(copies):
    for copy in copies:
        copy.start()
    return copies


def piece_copies(sources, rows_ref, sems):
    chunk = rows_ref.shape[0] // len(sources)
    return start_all(
        [
            pltpu.make_async_copy(source, rows_ref.at[pl.ds(m * chunk, chunk)], sems.at[m])
            for m, source in enumerate(sources)
        ]
    )


def group_copies(source, target, sems):
    count, number = target.shape[0], sems.shape[0]
    group = count // number
    return start_all(
        [
            pltpu.make_async_copy(
                source.at[pl.ds(i * group, group)], target.at[pl.ds(i * group, group)], sems.at[i]
            )
            for i in range(number)
        ]
    )


def hot_part(slot_ref, experts, part, slots):
    tokens = slot_ref.shape[1] // PARTS
    count = slots // PARTS
    columns = slice(part * tokens, (part + 1) * tokens)
    row = lax.broadcasted_iota(jnp.int32, (count, tokens), 0) + part * count
    return [row == slot_ref[e : e + 1, columns] for e in experts]


def dispatch(part, slot_ref, rows_ref, x_ref):
    local_count = slot_ref.shape[0]
    count = 2 * LINES * 2 * CAP // PARTS
    first_slot = part * count if x_ref.shape[1] > count else 0
    group = min(8, local_count)
    for first in range(0, local_count, group):
        experts = range(first, first + group)
        hot = jnp.concatenate(
            [h.astype(jnp.bfloat16) for h in hot_part(slot_ref, experts, part, count * PARTS)]
        )
        found = jnp.dot(hot, rows_ref[...], preferred_element_type=jnp.float32)
        found = found.astype(jnp.bfloat16)
        for i, e in enumerate(experts):
            x_ref[e, first_slot : first_slot + count] = found[i * count : (i + 1) * count]


def turn_kernel(w_ref, out_ref, w_here, out_here, w_sems, out_sems):
    weights = group_copies(w_ref, w_here, w_sems)
    group = w_here.shape[0] // len(weights)
    copies = []
    for i, weight in enumerate(weights):
        weight.wait()
        for e in range(i * group, (i + 1) * group):
            out_here[e] = w_here[e].T
        span = pl.ds(i * group, group)
        copies += start_all(
            [pltpu.make_async_copy(out_here.at[span], out_ref.at[span], out_sems.at[i])]
        )
    for copy in copies:
        copy.wait()


def first_kernel(slot_ref, gates_ref, *refs):
    pieces, (x_ref, grad_x_ref, slot_gates_ref) = refs[:4], refs[4:7]
    tokens_here, grads_here, token_sems, grad_sems = refs[7:]
    tokens = piece_copies([piece.at[0] for piece in pieces], tokens_here, token_sems)
    grads = piece_copies([piece.at[1] for piece in pieces], grads_here, grad_sems)
    for arrivals, rows_ref, target in (
        (tokens, tokens_here, x_ref),
        (grads, grads_here, grad_x_ref),
    ):
        for copy in arrivals:
            copy.wait()
        dispatch(0, slot_ref, rows_ref, target)
    local_count, slots, lanes = slot_gates_ref.shape
    tokens, count = slot_ref.shape[1] // PARTS, slots // PARTS
    for e in range(local_count):
        for part in range(PARTS):
            gates = gates_ref[e : e + 1, part * tokens : (part + 1) * tokens]
            gate = jnp.where(hot_part(slot_ref, [e], part, slots)[0], gates, 0.0)
            slot_gates_ref[e, part * count : (part + 1) * count] = jnp.broadcast_to(
                jnp.sum(gate, axis=1, keepdims=True), (count, lanes)
            )


def finish_slots(index, slot_ref, pieces, first_ref, rows_ref, x_here, piece_sems, first_sem):
    sources = [piece.at[index] if len(piece.shape) == 3 else piece for piece in pieces]
    arrivals = piece_copies(sources, rows_ref, piece_sems)
    count = first_ref.shape[1]
    first = pltpu.make_async_copy(first_ref, x_here.at[:, pl.ds(0, count)], first_sem)
    first.start()

    def finish():
        for copy in arrivals:
            copy.wait()
        dispatch(1, slot_ref, rows_ref, x_here)
        first.wait()

    return finish


def multiply(x_ref, w_ref, here, out_ref, out_sems, weights=None, side=0):
    groups = out_sems.shape[0]
    group = x_ref.shape[0] // groups
    copies = []
    for i in range(groups):
        if weights is not None:
            weights[i].wait()
        for e in range(i * group, (i + 1) * group):
            here[e] = lax.dot_general(
                x_ref[e],
                w_ref[e],
                (((1,), (side,)), ((), ())),
                preferred_element_type=jnp.float32,
            )
        span = pl.ds(i * group, group)
        copies += start_all(
            [pltpu.make_async_copy(here.at[span], out_ref.at[span], out_sems.at[i])]
        )
    return copies


def load_kernel(w_ref, out_ref, sems):
    for copy in group_copies(w_ref, out_ref, sems):
        copy.wait()


def pre_kernel(slot_ref, *refs):
    pieces, refs = refs[:4], refs[4:]
    first_ref, gate_w, up_w, x_ref, gate_ref, up_ref = refs[:6]
    rows_here, x_here, up_w_here, gate_here, up_here = refs[6:11]
    piece_sems, first_sem, up_w_sems, x_sem, gate_sems, up_sems = refs[11:]
    finish = finish_slots(
        0, slot_ref, pieces, first_ref, rows_here, x_here, piece_sems, first_sem
    )
    up_ws = group_copies(up_w, up_w_here, up_w_sems)
    finish()
    copies = start_all([pltpu.make_async_copy(x_here, x_ref, x_sem)])
    copies += multiply(x_here, gate_w, gate_here, gate_ref, gate_sems)
    copies += multiply(x_here, up_w_here, up_here, up_ref, up_sems, up_ws)
    for copy in copies:
        copy.wait()


def down_kernel(slot_ref, *refs):
    pieces, refs = refs[:4], refs[4:]
    first_ref, down_w, raw_ref = refs[:3]
    rows_here, x_here, w_here, here, piece_sems, first_sem, w_sems, out_sems = refs[3:]
    finish = finish_slots(
        1, slot_ref, pieces, first_ref, rows_here, x_here, piece_sems, first_sem
    )
    weights = group_copies(down_w, w_here, w_sems)
    finish()
    for copy in multiply(x_here, w_here, here, raw_ref, out_sems, weights, 1):
        copy.wait()


def keep_row(row, e, rows_ref):
    count = row.shape[0] // PARTS
    for part in range(PARTS):
        rows_ref[part, e * count : (e + 1) * count] = row[part * count : (part + 1) * count]


def combine(slot_ref, experts, rows_ref, sum_ref, outs, slots):
    local_count = slot_ref.shape[0]
    tokens, count = slot_ref.shape[1] // PARTS, slots // PARTS
    copies = []
    for part in reversed(range(PARTS)):
        hot = jnp.concatenate(
            [h.astype(jnp.bfloat16) for h in hot_part(slot_ref, experts, part, slots)]
        )
        total = lax.dot_general(
            hot,
            rows_ref[part, experts[0] * count : (experts[-1] + 1) * count],
            (((0,), (0,)), ((), ())),
            preferred_element_type=jnp.float32,
        )
        place = slice(part * tokens, (part + 1) * tokens)
        if experts[0] > 0:
            total += sum_ref[place]
        if experts[-1] < local_count - 1:
            sum_ref[place] = total
        else:
            each = len(outs) // PARTS
            for i, (here, out, sem) in enumerate(outs[part * each : (part + 1) * each]):
                rows = tokens // each
                here[...] = total[i * rows : (i + 1) * rows].astype(jnp.bfloat16)
                copies += start_all([pltpu.make_async_copy(here, out, sem)])
    return copies


def load_half_kernel(gate_w, up_w, gate_out, up_out, gate_sems, up_sems):
    half = pl.ds(0, gate_out.shape[0])
    copies = group_copies(gate_w.at[half], gate_out, gate_sems)
    copies += group_copies(up_w.at[half], up_out, up_sems)
    for copy in copies:
        copy.wait()


def rows_kernel(slot_ref, *refs):
    slot_gates_ref, sources, refs = refs[0], refs[1:7], refs[7:]
    gate_first, up_first, gate_w, up_w, grads_ref = refs[:5]
    out_refs, refs = refs[5 : 5 + 2 * LINES], refs[5 + 2 * LINES :]
    inputs_here, gate_here, up_here, grads_here, rows_ref, sum_ref, outs_here = refs[:7]
    input_sems, gate_sems, up_sems, grad_sems, out_sems = refs[7:]
    local_count, slots, hidden = inputs_here.shape[1:]
    outs = [(outs_here.at[m], out, out_sems.at[m]) for m, out in enumerate(out_refs)]
    copies = []
    groups = input_sems.shape[1]
    group = local_count // groups
    half = gate_first.shape[0]
    rest = pl.ds(half, local_count - half)
    arrivals = []
    for i in range(groups):
        here = pl.ds(i * group, group)
        arrivals.append(
            start_all(
                [
                    pltpu.make_async_copy(
                        source.at[here], inputs_here.at[j, here], input_sems.at[j, i]
                    )
                    for j, source in enumerate(sources)
                ]
            )
        )
    gate_ws = group_copies(gate_w.at[rest], gate_here, gate_sems)
    up_ws = group_copies(up_w.at[rest], up_here, up_sems)
    for i in range(groups):
        for copy in arrivals[i]:
            copy.wait()
        for e in range(i * group, (i + 1) * group):
            pre_gate = inputs_here[0, e] + inputs_here[1, e]
            pre_up = inputs_here[2, e] + inputs_here[3, e]
            raw = inputs_here[4, e] + inputs_here[5, e]
            sigmoid = jax.nn.sigmoid(pre_gate)
            scaled = slot_gates_ref[e, :, :1] * raw * sigmoid
            grad_gate = (scaled * pre_up * (1.0 + pre_gate * (1.0 - sigmoid))).astype(jnp.bfloat16)
            grad_up = (scaled * pre_gate).astype(jnp.bfloat16)
            grads_here[e, :, :hidden] = grad_gate
            grads_here[e, :, hidden:] = grad_up
            if e < half:
                gate_e, up_e = gate_first[e], up_first[e]
            else:
                span = half // len(gate_ws)
                if (e - half) % span == 0:
                    gate_ws[(e - half) // span].wait()
                    up_ws[(e - half) // span].wait()
                gate_e, up_e = gate_here[e - half], up_here[e - half]
            row = jnp.dot(grad_gate, gate_e, preferred_element_type=jnp.float32)
            row += lax.dot_general(
                grad_up, up_e, (((1,), (1,)), ((), ())), preferred_element_type=jnp.float32
            )
            keep_row(row.astype(jnp.bfloat16), e, rows_ref)
        if (i + 1) % (groups // 2) == 0:
            last = (i + 1) * group
            experts = range(last - local_count // 2, last)
            here = pl.ds(experts[0], len(experts))
            copies += start_all(
                [
                    pltpu.make_async_copy(
                        grads_here.at[here], grads_ref.at[here], grad_sems.at[i // (groups // 2)]
                    )
                ]
            )
            copies += combine(slot_ref, experts, rows_ref, sum_ref, outs, slots)
    for copy in copies:
        copy.wait()


def weight_kernel(x_ref, grads_ref, *refs):
    gate_out_ref, up_out_ref = refs[-2:]
    hidden = gate_out_ref.shape[-1]
    for i in range(x_ref.shape[0]):
        found = lax.dot_general(
            x_ref[i], grads_ref[i], (((0,), (0,)), ((), ())), preferred_element_type=jnp.float32
        ).astype(jnp.bfloat16)
        gate_out_ref[i] = found[:, :hidden]
        up_out_ref[i] = found[:, hidden:]


def in_hbm(value):
    return pltpu.with_memory_space_constraint(value, pltpu.HBM)


def in_vmem(value):
    return pltpu.with_memory_space_constraint(value, pltpu.VMEM)


def params(mib):
    return pltpu.CompilerParams(vmem_limit_bytes=mib * 1024 * 1024)


def cost(flops, moved):
    return pl.CostEstimate(flops=int(flops), bytes_accessed=int(moved), transcendentals=0)


def gather_body(tokens, out_grad, route_gates, expert_ids, w_gate, w_up, w_down):
    ep_count = 2 * LINES
    local_count, half_width, hidden = w_gate.shape
    block_rows, top_count = expert_ids.shape
    chunk = 2 * block_rows
    token_count = ep_count * chunk
    slots = 2 * ep_count * CAP
    part_slots, part_tokens = slots // PARTS, token_count // PARTS
    place = lax.axis_index("ep")
    here, side = place // 2, place % 2
    at_end = (here == 0) | (here == LINES - 1)
    bf16, f32 = jnp.bfloat16, jnp.float32
    memory = pl.BlockSpec(memory_space=pl.ANY)
    smem = pl.BlockSpec(memory_space=pltpu.SMEM)
    vmem = pl.BlockSpec(memory_space=pltpu.VMEM)
    copies = pltpu.SemaphoreType.DMA

    own_info = jnp.concatenate([expert_ids.astype(bf16), route_gates], axis=1).T
    info = jnp.zeros((ep_count, 2 * top_count, chunk), bf16)
    info = lax.dynamic_update_slice(
        info, own_info[None], (place, 0, lax.axis_index("dp") * block_rows)
    )
    line_order = jnp.asarray(ORDERS, jnp.int32)[here]
    order = (2 * line_order[:, None] + jnp.stack([side, 1 - side])[None, :]).reshape(-1)

    weight_bytes = local_count * half_width * hidden * 2
    matmul_flops = 2 * local_count * slots * half_width * hidden
    hot_flops = local_count * slots * half_width * token_count
    groups = 4
    piece_sems, w_sems = copies((ep_count // PARTS,)), copies((groups,))
    rows_here = pltpu.VMEM((part_tokens, half_width), bf16)
    x_shape = jax.ShapeDtypeStruct((local_count, slots, half_width), bf16)
    x_here = pltpu.VMEM(x_shape.shape, bf16)
    w_here, down_here = pltpu.VMEM(w_gate.shape, bf16), pltpu.VMEM(w_down.shape, bf16)
    pre_shape = jax.ShapeDtypeStruct((local_count, slots, hidden), f32)
    in_hbm_shape = pltpu.HBM(pre_shape.shape, f32)
    pre_here = pltpu.VMEM(pre_shape.shape, f32)
    batch = 2 if local_count % 2 == 0 else 1

    def batched(*shape):
        return pl.BlockSpec((batch,) + shape, lambda e: (e, 0, 0))

    def turned(weights):
        _, rows, columns = weights.shape
        shape = (local_count, columns, rows)
        return pl.pallas_call(
            turn_kernel,
            out_shape=pltpu.HBM(shape, bf16),
            in_specs=[memory],
            out_specs=memory,
            scratch_shapes=[w_here, pltpu.VMEM(shape, bf16), w_sems, w_sems],
            compiler_params=params(26),
            cost_estimate=cost(0, 2 * weight_bytes),
            name="turn",
        )(in_hbm(weights))

    made = {}

    def beside_gather(turn, info, pieces):
        if turn == 0:
            (gate_w,) = tie([w_gate], info)
            made["gate"] = turned(gate_w)
            return [made["gate"]]
        if turn == 2:
            (gate_w,) = tie([w_gate], *pieces)
            made["loaded"] = pl.pallas_call(
                load_kernel,
                out_shape=pltpu.VMEM(w_gate.shape, bf16),
                in_specs=[memory],
                out_specs=memory,
                scratch_shapes=[w_sems],
                compiler_params=params(24),
                cost_estimate=cost(0, weight_bytes),
                name="load",
            )(in_hbm(gate_w))
            return []
        made["slots"], made["gates"] = pl.pallas_call(
            functools.partial(route_kernel, top_count=top_count, block_rows=block_rows),
            out_shape=(
                jax.ShapeDtypeStruct((local_count, token_count), jnp.int32),
                jax.ShapeDtypeStruct((local_count, token_count), f32),
            ),
            in_specs=[smem, smem, vmem],
            out_specs=(vmem, vmem),
            compiler_params=params(16),
            cost_estimate=cost(1e7, 1e6),
            name="route",
        )(order, (place * local_count).reshape(1), info)
        part_shape = jax.ShapeDtypeStruct((local_count, part_slots, half_width), bf16)
        made["x"], made["grad_x"], made["slot_gates"] = pl.pallas_call(
            first_kernel,
            out_shape=(
                part_shape,
                part_shape,
                jax.ShapeDtypeStruct((local_count, slots, 128), f32),
            ),
            in_specs=[vmem] * 2 + [memory] * 4,
            out_specs=(vmem,) * 3,
            scratch_shapes=[rows_here, rows_here, piece_sems, piece_sems],
            compiler_params=params(32),
            cost_estimate=cost(hot_flops, weight_bytes / 2),
            name="first_slots",
        )(made["slots"], made["gates"], *pieces)
        return [made["x"], made["grad_x"]]

    pieces = gather_rows(jnp.stack([tokens, out_grad]), info, at_end, beside_gather)
    slot_of = made["slots"]

    x, gate_part, up_part = pl.pallas_call(
        pre_kernel,
        out_shape=(x_shape, in_hbm_shape, in_hbm_shape),
        in_specs=[vmem] + [memory] * 5 + [vmem, memory],
        out_specs=(memory,) * 3,
        scratch_shapes=[rows_here, x_here, w_here, pre_here, pre_here]
        + [piece_sems, copies, w_sems, copies, w_sems, w_sems],
        compiler_params=params(24),
        cost_estimate=cost(hot_flops / 2 + 2 * matmul_flops, 2.8 * weight_bytes),
        name="pre",
    )(
        slot_of,
        *pieces[4:8],
        made["x"],
        in_vmem(made["loaded"]),
        in_hbm(w_up),
    )
    grad_pieces = tie(pieces[8:], x)
    raw_part = pl.pallas_call(
        down_kernel,
        out_shape=in_hbm_shape,
        in_specs=[vmem] + [memory] * 6,
        out_specs=memory,
        scratch_shapes=[rows_here, x_here, down_here, pre_here]
        + [piece_sems, copies, w_sems, w_sems],
        compiler_params=params(19),
        cost_estimate=cost(hot_flops / 2 + matmul_flops, 1.4 * weight_bytes),
        name="down",
    )(slot_of, *pieces[4:6], *grad_pieces, made["grad_x"], in_hbm(w_down))
    gate_other, up_other = across_cores(gate_part), across_cores(up_part)
    raw_other = across_cores(raw_part)
    half = local_count // 2
    gate_half, up_half = (half, hidden, half_width), (half, half_width, hidden)
    gate_w, up_w = tie((made["gate"], w_up), raw_part, gate_other, up_other)
    gate_first, up_first = pl.pallas_call(
        load_half_kernel,
        out_shape=(pltpu.VMEM(gate_half, bf16), pltpu.VMEM(up_half, bf16)),
        in_specs=[memory] * 2,
        out_specs=(memory,) * 2,
        scratch_shapes=[w_sems, w_sems],
        compiler_params=params(40),
        cost_estimate=cost(0, weight_bytes),
        name="load_half",
    )(in_hbm(gate_w), in_hbm(up_w))
    grads, *partial = pl.pallas_call(
        rows_kernel,
        out_shape=(jax.ShapeDtypeStruct((local_count, slots, 2 * hidden), bf16),)
        + (jax.ShapeDtypeStruct((chunk, half_width), bf16),) * ep_count,
        in_specs=[vmem] * 2 + [memory] * 6 + [vmem] * 2 + [memory] * 2,
        out_specs=(memory,) * (1 + ep_count),
        scratch_shapes=[
            pltpu.VMEM((6,) + pre_shape.shape, f32),
            pltpu.VMEM(gate_half, bf16),
            pltpu.VMEM(up_half, bf16),
            pltpu.VMEM((local_count, slots, 2 * hidden), bf16),
            pltpu.VMEM((PARTS, local_count * part_slots, half_width), bf16),
            pltpu.VMEM((token_count, half_width), f32),
            pltpu.VMEM((ep_count, chunk, half_width), bf16),
            copies((6, 2 * groups)),
            w_sems,
            w_sems,
            copies((2,)),
            copies((ep_count,)),
        ],
        compiler_params=params(40),
        cost_estimate=cost(2 * matmul_flops + hot_flops, 2 * weight_bytes),
        name="rows",
    )(
        slot_of,
        made["slot_gates"],
        *[
            in_hbm(value)
            for value in (gate_part, gate_other, up_part, up_other, raw_part, raw_other)
        ],
        in_vmem(gate_first),
        in_vmem(up_first),
        in_hbm(made["gate"]),
        in_hbm(w_up),
    )

    turns = LINES
    group = local_count // turns
    weight_shape = jax.ShapeDtypeStruct(w_gate.shape, bf16)
    weight_grads = []

    def block_of(first, *shape):
        return pl.BlockSpec((1,) + shape, lambda e: (first + e, 0, 0))

    def meanwhile(turn, values):
        first = turn * group
        operands = [x, grads]
        operands = tie(operands, *(held or partial))
        weight_grads[:] = pl.pallas_call(
            weight_kernel,
            grid=(group,),
            out_shape=(weight_shape, weight_shape),
            in_specs=[block_of(first, slots, half_width), block_of(first, slots, 2 * hidden)]
            + [memory] * len(weight_grads),
            out_specs=(block_of(first, half_width, hidden), block_of(first, half_width, hidden)),
            input_output_aliases={2 + i: i for i in range(len(weight_grads))},
            compiler_params=params(32),
            cost_estimate=cost(2 * matmul_flops / turns, 2.5 * weight_bytes / turns),
            name="weight_grads",
        )(*operands, *weight_grads)
        *values, weight_grads[0], weight_grads[1] = tie([*values, *weight_grads])
        held[:] = values
        return values

    held = []
    grad_input = scatter_sums(partial, meanwhile)
    return (grad_input, *weight_grads)


def solution(mesh):
    in_specs = (
        P(("groups", "ep"), "dp"),
        P(("groups", "ep"), "dp"),
        P(("groups", "ep", "dp"), None),
        P(("groups", "ep", "dp"), None),
        P("ep", "dp", None),
        P("ep", "dp", None),
        P("ep", None, "dp"),
    )
    out_specs = (
        P(("groups", "ep"), "dp"),
        P(("groups", "ep"), "dp", None),
        P(("groups", "ep"), "dp", None),
    )
    ep_count = mesh.shape["ep"]
    body = gather_body if ep_count == 2 * LINES else exchange_body
    return jax.shard_map(body, mesh=mesh, in_specs=in_specs, out_specs=out_specs, check_vma=False)
```

```python
import functools

import jax
import jax.numpy as jnp
from jax import lax
from jax.experimental import pallas as pl
from jax.experimental.pallas import tpu as pltpu
from jax.sharding import PartitionSpec as P

CAP = 6


def route_slots(expert_ids, experts, stride, offset):
    flattened = expert_ids.reshape(-1)
    onehot = (flattened[:, None] == jnp.arange(experts, dtype=jnp.int32)[None, :]).astype(jnp.int32)
    ranking = jnp.sum(onehot * (jnp.cumsum(onehot, axis=0) - 1), axis=1)
    return flattened * stride + offset + ranking


def fill_slots(values, slot_ids, slot_count):
    zeroed = jnp.zeros((slot_count,) + values.shape[1:], values.dtype)
    return zeroed.at[slot_ids].set(values)


def swiglu_back(pre_gate, pre_up, raw_down, gate_rows):
    grad_hidden = gate_rows.astype(jnp.float32)[..., None] * raw_down
    sigmoid = jax.nn.sigmoid(pre_gate)
    grad_gate_pre = (grad_hidden * pre_up * sigmoid * (1.0 + pre_gate * (1.0 - sigmoid))).astype(
        jnp.bfloat16
    )
    grad_up_pre = (grad_hidden * pre_gate * sigmoid).astype(jnp.bfloat16)
    return (grad_gate_pre, grad_up_pre)


def share_pre_grads(grad_gate_pre, grad_up_pre):
    return (
        lax.all_gather(grad_gate_pre, "dp", axis=2, tiled=True),
        lax.all_gather(grad_up_pre, "dp", axis=2, tiled=True),
    )


def weight_terms(shaped_rows, both_gate, both_up):
    grad_gate_w = jnp.einsum(
        "nlbcd,nlbcf->ldf", shaped_rows, both_gate, preferred_element_type=jnp.float32
    )
    grad_up_w = jnp.einsum(
        "nlbcd,nlbcf->ldf", shaped_rows, both_up, preferred_element_type=jnp.float32
    )
    return (grad_gate_w.astype(jnp.bfloat16), grad_up_w.astype(jnp.bfloat16))


def expert_work(token_rows, grad_rows, gate_rows, w_gate, w_up, w_down):
    full_gate, full_up, full_down = (
        lax.all_gather(w_gate, "dp", axis=1, tiled=True),
        lax.all_gather(w_up, "dp", axis=1, tiled=True),
        lax.all_gather(w_down, "dp", axis=2, tiled=True),
    )
    pre_gate = jnp.einsum(
        "nlcd,ldf->nlcf", token_rows, full_gate, preferred_element_type=jnp.float32
    )
    pre_up = jnp.einsum("nlcd,ldf->nlcf", token_rows, full_up, preferred_element_type=jnp.float32)
    raw_down = jnp.einsum(
        "nlcd,lfd->nlcf", grad_rows, full_down, preferred_element_type=jnp.float32
    )
    grad_gate_pre, grad_up_pre = swiglu_back(pre_gate, pre_up, raw_down, gate_rows)
    row_grad = (
        jnp.einsum("nlcf,ldf->nlcd", grad_gate_pre, full_gate, preferred_element_type=jnp.float32)
        + jnp.einsum("nlcf,ldf->nlcd", grad_up_pre, full_up, preferred_element_type=jnp.float32)
    ).astype(jnp.bfloat16)
    return (row_grad, grad_gate_pre, grad_up_pre)


def exchange_body(tokens, out_grad, route_gates, expert_ids, w_gate, w_up, w_down):
    ep_count = lax.axis_size("ep")
    local_count = w_gate.shape[0]
    experts = local_count * ep_count
    block_rows, top_count = expert_ids.shape
    capacity = CAP
    half_width = tokens.shape[1]
    feature_width = 2 * half_width
    pair_ids = lax.all_gather(expert_ids, "dp", axis=0, tiled=True)
    first_slots = route_slots(pair_ids[:block_rows], experts, 2 * capacity, 0)
    second_slots = route_slots(pair_ids[block_rows:], experts, 2 * capacity, capacity)
    slot_ids = jnp.concatenate([first_slots, second_slots])
    own_slots = lax.dynamic_index_in_dim(
        slot_ids.reshape(2, block_rows * top_count), lax.axis_index("dp"), 0, keepdims=False
    )
    token_of = jnp.arange(2 * block_rows * top_count, dtype=jnp.int32) // top_count
    slot_count = experts * 2 * capacity
    send_rows = fill_slots(tokens[token_of], slot_ids, slot_count).reshape(
        ep_count, local_count * 2 * capacity, half_width
    )
    send_grads = fill_slots(out_grad[token_of], slot_ids, slot_count).reshape(
        ep_count, local_count * 2 * capacity, half_width
    )
    send_gates = fill_slots(route_gates.reshape(-1), own_slots, slot_count).reshape(
        ep_count, local_count * 2 * capacity
    )
    recv_rows, recv_grads, recv_gates = (
        lax.all_to_all(send_rows, "ep", split_axis=0, concat_axis=0, tiled=True),
        lax.all_to_all(send_grads, "ep", split_axis=0, concat_axis=0, tiled=True),
        lax.all_to_all(send_gates, "ep", split_axis=0, concat_axis=0, tiled=True),
    )
    shaped_rows = recv_rows.reshape(ep_count, local_count, 2, capacity, half_width)
    shaped_grads = recv_grads.reshape(ep_count, local_count, 2, capacity, half_width)
    shaped_gates = recv_gates.reshape(ep_count, local_count, 2, capacity)
    joined_rows, joined_grads = (
        lax.all_to_all(shaped_rows, "dp", split_axis=2, concat_axis=4, tiled=True),
        lax.all_to_all(shaped_grads, "dp", split_axis=2, concat_axis=4, tiled=True),
    )
    token_rows = joined_rows.reshape(ep_count, local_count, capacity, feature_width)
    grad_rows = joined_grads.reshape(ep_count, local_count, capacity, feature_width)
    gate_rows = lax.dynamic_index_in_dim(shaped_gates, lax.axis_index("dp"), 2, keepdims=False)
    row_grad, grad_gate_pre, grad_up_pre = expert_work(
        token_rows, grad_rows, gate_rows, w_gate, w_up, w_down
    )
    both_gate, both_up = share_pre_grads(
        grad_gate_pre.reshape(ep_count, local_count, 1, capacity, -1),
        grad_up_pre.reshape(ep_count, local_count, 1, capacity, -1),
    )
    spread = lax.all_to_all(
        row_grad.reshape(ep_count, local_count, 1, capacity, feature_width),
        "dp",
        split_axis=4,
        concat_axis=2,
        tiled=True,
    )
    grad_gate_w, grad_up_w = weight_terms(shaped_rows, both_gate, both_up)
    returned = lax.all_to_all(
        spread.reshape(ep_count, local_count * 2 * capacity, half_width),
        "ep",
        split_axis=0,
        concat_axis=0,
        tiled=True,
    )
    returned = returned.reshape(slot_count, half_width)
    per_route = (
        returned[slot_ids].astype(jnp.float32).reshape(2 * block_rows, top_count, half_width)
    )
    grad_input = jnp.sum(per_route, axis=1).astype(jnp.bfloat16)
    return (grad_input, grad_gate_w, grad_up_w)


ORDERS = ((0, 1, 2, 3), (1, 0, 2, 3), (2, 3, 1, 0), (3, 2, 1, 0))
LINES = len(ORDERS)
PARTS = 2
HALVES = 2
OUTER = ((0, 1), (1, 0), (2, 3), (3, 2))
INNER = ((1, 2), (2, 1))
TO_END = ((1, 0), (2, 3))
FROM_END = ((0, 1), (3, 2))


def along_line(value, moves):
    pairs = [(2 * a + side, 2 * b + side) for a, b in moves for side in range(2)]
    return lax.ppermute(value, "ep", pairs)


def across_pair(value):
    return lax.ppermute(value, "ep", [(i, i ^ 1) for i in range(2 * LINES)])


def across_cores(value):
    return lax.ppermute(value, "dp", [(0, 1), (1, 0)])


def tie(values, *others):
    values = list(values)
    return list(lax.optimization_barrier(tuple(values) + tuple(others))[: len(values)])


def gather_rows(rows, info, at_end, meanwhile):
    def widen(info, bits):
        came = [
            lax.ppermute(info, "ep", [(i, i ^ bit) for i in range(2 * LINES)]) for bit in bits
        ]
        return functools.reduce(jnp.add, came, info)

    outer, inner, other = along_line(rows, OUTER), along_line(rows, INNER), across_pair(rows)
    info = widen(info + across_cores(info), [1])
    info = widen(info, [2, 4, 6])
    outer, inner, other, info = tie((outer, inner, other, info))
    pieces = [rows, other]

    second, third = along_line(inner, TO_END), along_line(outer, INNER)
    other = across_pair(outer)
    second, third, other = tie((second, third, other))
    pieces += [outer, other]

    middle = jnp.where(at_end, second, inner)
    last, other = along_line(third, TO_END), across_pair(middle)
    done = meanwhile(0, info, pieces)
    last, other = tie((last, other), *done)
    pieces += [middle, other]

    meanwhile(1, info, [last, other])
    for part in range(2):
        far = jnp.where(at_end, last[part], third[part])
        pieces += [far, across_pair(far)]
        last, third = tie((last, third))
    return pieces


def scatter_sums(partial, meanwhile):
    f32, bf16 = jnp.float32, jnp.bfloat16

    def own_side(m, other):
        return partial[2 * m].astype(f32) + other.astype(f32)

    other = across_pair(partial[7])
    (other,) = meanwhile(0, [other])
    far = own_side(3, other)
    outward, other = along_line(far.astype(bf16), FROM_END), across_pair(partial[5])
    outward, other = meanwhile(1, [outward, other])
    middle = own_side(2, other)
    crossed = along_line((far + outward.astype(f32)).astype(bf16), INNER)
    outward, other = along_line(middle.astype(bf16), FROM_END), across_pair(partial[3])
    crossed, outward, other = meanwhile(2, [crossed, outward, other])
    near = own_side(1, other) + crossed.astype(f32)
    inner = along_line((middle + outward.astype(f32)).astype(bf16), INNER)
    outer, other = along_line(near.astype(bf16), OUTER), across_pair(partial[1])
    inner, outer, other = meanwhile(3, [inner, outer, other])
    total = own_side(0, other) + outer.astype(f32) + inner.astype(f32)
    return total.astype(bf16)


def route_kernel(order_ref, base_ref, info_ref, slot_ref, gate_ref, *, top_count, block_rows):
    local_count = slot_ref.shape[0]
    chunk = info_ref.shape[2]
    row = lax.broadcasted_iota(jnp.int32, (chunk, chunk), 0)
    column = lax.broadcasted_iota(jnp.int32, (chunk, chunk), 1)
    before = ((row < column) & (row // block_rows == column // block_rows)).astype(jnp.bfloat16)
    lane = lax.broadcasted_iota(jnp.int32, (local_count, chunk), 1)
    expert = (base_ref[0] + lax.broadcasted_iota(jnp.int32, (local_count, chunk), 0)).astype(
        jnp.float32
    )
    for piece in range(info_ref.shape[0]):
        info = info_ref[order_ref[piece]].astype(jnp.float32)
        named = jnp.zeros((local_count, chunk), jnp.float32)
        gate = jnp.zeros((local_count, chunk), jnp.float32)
        for k in range(top_count):
            match = info[k : k + 1, :] == expert
            named = jnp.where(match, 1.0, named)
            gate = jnp.where(match, info[top_count + k : top_count + k + 1, :], gate)
        rank = jnp.dot(
            named.astype(jnp.bfloat16), before, preferred_element_type=jnp.float32
        ).astype(jnp.int32)
        block = piece * (chunk // block_rows) + lane // block_rows
        columns = pl.ds(piece * chunk, chunk)
        slot_ref[:, columns] = jnp.where(named > 0.5, block * CAP + rank, -1)
        gate_ref[:, columns] = gate


def start_all(copies):
    for copy in copies:
        copy.start()
    return copies


def piece_copies(sources, rows_ref, sems):
    chunk = rows_ref.shape[0] // len(sources)
    return start_all(
        [
            pltpu.make_async_copy(source, rows_ref.at[pl.ds(m * chunk, chunk)], sems.at[m])
            for m, source in enumerate(sources)
        ]
    )


def group_copies(source, target, sems):
    count, number = target.shape[0], sems.shape[0]
    group = count // number
    return start_all(
        [
            pltpu.make_async_copy(
                source.at[pl.ds(i * group, group)], target.at[pl.ds(i * group, group)], sems.at[i]
            )
            for i in range(number)
        ]
    )


def hot_part(slot_ref, experts, part, slots):
    tokens = slot_ref.shape[1] // PARTS
    count = slots // PARTS
    columns = slice(part * tokens, (part + 1) * tokens)
    row = lax.broadcasted_iota(jnp.int32, (count, tokens), 0) + part * count
    return [row == slot_ref[e : e + 1, columns] for e in experts]


def dispatch(part, slot_ref, rows_ref, x_ref, start=0):
    local_count = x_ref.shape[0]
    count = 2 * LINES * 2 * CAP // PARTS
    first_slot = part * count if x_ref.shape[1] > count else 0
    group = min(8, local_count)
    for first in range(0, local_count, group):
        experts = range(start + first, start + first + group)
        hot = jnp.concatenate(
            [h.astype(jnp.bfloat16) for h in hot_part(slot_ref, experts, part, count * PARTS)]
        )
        found = jnp.dot(hot, rows_ref[...], preferred_element_type=jnp.float32)
        found = found.astype(jnp.bfloat16)
        for i, e in enumerate(experts):
            x_ref[e - start, first_slot : first_slot + count] = found[i * count : (i + 1) * count]


def first_kernel(slot_ref, gates_ref, *refs):
    pieces, (x_ref, grad_x_ref, slot_gates_ref) = refs[:4], refs[4:7]
    tokens_here, grads_here, token_sems, grad_sems = refs[7:]
    tokens = piece_copies([piece.at[0] for piece in pieces], tokens_here, token_sems)
    grads = piece_copies([piece.at[1] for piece in pieces], grads_here, grad_sems)
    for arrivals, rows_ref, target in (
        (tokens, tokens_here, x_ref),
        (grads, grads_here, grad_x_ref),
    ):
        for copy in arrivals:
            copy.wait()
        dispatch(0, slot_ref, rows_ref, target)
    local_count, slots, lanes = slot_gates_ref.shape
    tokens, count = slot_ref.shape[1] // PARTS, slots // PARTS
    for e in range(local_count):
        for part in range(PARTS):
            gates = gates_ref[e : e + 1, part * tokens : (part + 1) * tokens]
            gate = jnp.where(hot_part(slot_ref, [e], part, slots)[0], gates, 0.0)
            slot_gates_ref[e, part * count : (part + 1) * count] = jnp.broadcast_to(
                jnp.sum(gate, axis=1, keepdims=True), (count, lanes)
            )


def finish_slots(
    index, slot_ref, pieces, first_ref, rows_ref, x_here, piece_sems, first_sem, start=0
):
    sources = [piece.at[index] if len(piece.shape) == 3 else piece for piece in pieces]
    arrivals = piece_copies(sources, rows_ref, piece_sems)
    experts = pl.ds(start, x_here.shape[0])
    first = pltpu.make_async_copy(
        first_ref.at[experts], x_here.at[:, pl.ds(0, first_ref.shape[1])], first_sem
    )
    first.start()

    def finish():
        for copy in arrivals:
            copy.wait()
        dispatch(1, slot_ref, rows_ref, x_here, start)
        first.wait()

    return finish


def multiply(x_ref, w_ref, here, out_refs, out_sems, weights=None, side=0):
    groups = out_sems.shape[0]
    group = x_ref.shape[0] // groups
    copies = []
    for i in range(groups):
        if weights is not None:
            weights[i].wait()
        for e in range(i * group, (i + 1) * group):
            here[e] = lax.dot_general(
                x_ref[e],
                w_ref[e],
                (((1,), (side,)), ((), ())),
                preferred_element_type=jnp.float32,
            )
        span, each = pl.ds(i * group, group), groups // len(out_refs)
        target = out_refs[i // each].at[pl.ds(i % each * group, group)]
        copies += start_all([pltpu.make_async_copy(here.at[span], target, out_sems.at[i])])
    return copies


def load_kernel(w_ref, out_ref, sems):
    for copy in group_copies(w_ref, out_ref, sems):
        copy.wait()


def pre_kernel(slot_ref, *refs):
    pieces, refs = refs[:4], refs[4:]
    first_ref, gate_w, up_w, x_ref = refs[:4]
    gate_refs, up_refs = refs[4 : 4 + HALVES], refs[4 + HALVES : 4 + 2 * HALVES]
    refs = refs[4 + 2 * HALVES :]
    rows_here, x_here, up_w_here, gate_here, up_here = refs[:5]
    piece_sems, first_sem, up_w_sems, x_sem, gate_sems, up_sems = refs[5:]
    finish = finish_slots(
        0, slot_ref, pieces, first_ref, rows_here, x_here, piece_sems, first_sem
    )
    up_ws = group_copies(up_w, up_w_here, up_w_sems)
    finish()
    copies = start_all([pltpu.make_async_copy(x_here, x_ref, x_sem)])
    copies += multiply(x_here, gate_w, gate_here, gate_refs, gate_sems)
    copies += multiply(x_here, up_w_here, up_here, up_refs, up_sems, up_ws)
    for copy in copies:
        copy.wait()


def down_kernel(start, slot_ref, *refs):
    pieces, refs = refs[:4], refs[4:]
    first_ref, down_w, raw_ref = refs[:3]
    rows_here, x_here, w_here, here, piece_sems, first_sem, w_sems, out_sems = refs[3:]
    finish = finish_slots(
        1, slot_ref, pieces, first_ref, rows_here, x_here, piece_sems, first_sem, start
    )
    weights = group_copies(down_w.at[pl.ds(start, x_here.shape[0])], w_here, w_sems)
    finish()
    for copy in multiply(x_here, w_here, here, [raw_ref], out_sems, weights, 1):
        copy.wait()


def keep_row(row, e, rows_ref):
    count = row.shape[0] // PARTS
    for part in range(PARTS):
        rows_ref[part, e * count : (e + 1) * count] = row[part * count : (part + 1) * count]


def sum_rows(part, start, local_count, slot_ref, rows, slots):
    experts = range(start, start + local_count)
    hot = jnp.concatenate(
        [h.astype(jnp.bfloat16) for h in hot_part(slot_ref, experts, part, slots)]
    )
    return lax.dot_general(
        hot, rows, (((0,), (0,)), ((), ())), preferred_element_type=jnp.float32
    )


def give_out(total, outs_here, out_refs, out_sems):
    rows = total.shape[0] // len(out_refs)
    for i in range(len(out_refs)):
        outs_here[i] = total[i * rows : (i + 1) * rows].astype(jnp.bfloat16)
    return start_all(
        [
            pltpu.make_async_copy(outs_here.at[i], out_ref, out_sems.at[i])
            for i, out_ref in enumerate(out_refs)
        ]
    )


def rows_kernel(start, slot_ref, slot_gates_ref, *refs):
    sources, gate_w, up_w, refs = refs[:6], refs[6], refs[7], refs[8:]
    last = start > 0
    if last:
        before_ref, refs = refs[0], refs[1:]
    grads_ref, near_ref, refs = refs[0], refs[1], refs[2:]
    if last:
        out_refs, refs = refs[:LINES], refs[LINES:]
        outs_here, out_sems = refs[-2:]
    else:
        sum_ref, refs = refs[0], refs[1:]
    inputs_here, gate_here, up_here, grads_here, rows_ref = refs[:5]
    input_sems, gate_sems, up_sems, grads_sem, near_sem = refs[5:10]
    local_count, slots, hidden = inputs_here.shape[1:]
    groups = input_sems.shape[1]
    group = local_count // groups
    arrivals = []
    for i in range(groups):
        here, there = pl.ds(i * group, group), pl.ds(start + i * group, group)
        moves = [
            pltpu.make_async_copy(source.at[here], inputs_here.at[j, here], input_sems.at[j, i])
            for j, source in enumerate(sources)
        ]
        moves += [
            pltpu.make_async_copy(gate_w.at[there], gate_here.at[here], gate_sems.at[i]),
            pltpu.make_async_copy(up_w.at[there], up_here.at[here], up_sems.at[i]),
        ]
        arrivals.append(start_all(moves))
    for i in range(groups):
        for copy in arrivals[i]:
            copy.wait()
        for e in range(i * group, (i + 1) * group):
            pre_gate = inputs_here[0, e] + inputs_here[1, e]
            pre_up = inputs_here[2, e] + inputs_here[3, e]
            raw = inputs_here[4, e] + inputs_here[5, e]
            sigmoid = jax.nn.sigmoid(pre_gate)
            scaled = slot_gates_ref[start + e, :, :1] * raw * sigmoid
            grad_gate = (scaled * pre_up * (1.0 + pre_gate * (1.0 - sigmoid))).astype(jnp.bfloat16)
            grad_up = (scaled * pre_gate).astype(jnp.bfloat16)
            grads_here[e, :, :hidden] = grad_gate
            grads_here[e, :, hidden:] = grad_up
            turned = (((1,), (1,)), ((), ()))
            row = lax.dot_general(
                grad_gate, gate_here[e], turned, preferred_element_type=jnp.float32
            )
            row += lax.dot_general(grad_up, up_here[e], turned, preferred_element_type=jnp.float32)
            keep_row(row.astype(jnp.bfloat16), e, rows_ref)
    copies = start_all(
        [
            pltpu.make_async_copy(grads_here, grads_ref, grads_sem),
            pltpu.make_async_copy(rows_ref.at[0], near_ref, near_sem),
        ]
    )
    total = sum_rows(1, start, local_count, slot_ref, rows_ref[1], slots)
    if last:
        copies += give_out(total + before_ref[...], outs_here, out_refs, out_sems)
    else:
        sum_ref[...] = total
    for copy in copies:
        copy.wait()


def near_kernel(slot_ref, *refs):
    rows_refs, out_refs = refs[:HALVES], refs[HALVES : HALVES + LINES]
    rows_here, outs_here, row_sems, out_sems = refs[HALVES + LINES :]
    count = rows_here.shape[0] // HALVES
    copies = start_all(
        [
            pltpu.make_async_copy(ref, rows_here.at[pl.ds(i * count, count)], row_sems.at[i])
            for i, ref in enumerate(rows_refs)
        ]
    )
    for copy in copies:
        copy.wait()
    local_count = slot_ref.shape[0]
    slots = PARTS * rows_here.shape[0] // local_count
    total = sum_rows(0, 0, local_count, slot_ref, rows_here[...], slots)
    for copy in give_out(total, outs_here, out_refs, out_sems):
        copy.wait()


def weight_kernel(x_ref, grads_ref, *refs):
    gate_out_ref, up_out_ref = refs[-2:]
    hidden = gate_out_ref.shape[-1]
    for i in range(x_ref.shape[0]):
        found = lax.dot_general(
            x_ref[i], grads_ref[i], (((0,), (0,)), ((), ())), preferred_element_type=jnp.float32
        ).astype(jnp.bfloat16)
        gate_out_ref[i] = found[:, :hidden]
        up_out_ref[i] = found[:, hidden:]


def in_hbm(value):
    return pltpu.with_memory_space_constraint(value, pltpu.HBM)


def in_vmem(value):
    return pltpu.with_memory_space_constraint(value, pltpu.VMEM)


def params(mib):
    return pltpu.CompilerParams(vmem_limit_bytes=mib * 1024 * 1024)


def cost(flops, moved):
    return pl.CostEstimate(flops=int(flops), bytes_accessed=int(moved), transcendentals=0)


def gather_body(tokens, out_grad, route_gates, expert_ids, w_gate, w_up, w_down):
    ep_count = 2 * LINES
    local_count, half_width, hidden = w_gate.shape
    block_rows, top_count = expert_ids.shape
    chunk = 2 * block_rows
    token_count = ep_count * chunk
    slots = 2 * ep_count * CAP
    part_slots, part_tokens = slots // PARTS, token_count // PARTS
    place = lax.axis_index("ep")
    here, side = place // 2, place % 2
    at_end = (here == 0) | (here == LINES - 1)
    bf16, f32 = jnp.bfloat16, jnp.float32
    memory = pl.BlockSpec(memory_space=pl.ANY)
    smem = pl.BlockSpec(memory_space=pltpu.SMEM)
    vmem = pl.BlockSpec(memory_space=pltpu.VMEM)
    copies = pltpu.SemaphoreType.DMA

    own_info = jnp.concatenate([expert_ids.astype(bf16), route_gates], axis=1).T
    info = jnp.zeros((ep_count, 2 * top_count, chunk), bf16)
    info = lax.dynamic_update_slice(
        info, own_info[None], (place, 0, lax.axis_index("dp") * block_rows)
    )
    line_order = jnp.asarray(ORDERS, jnp.int32)[here]
    order = (2 * line_order[:, None] + jnp.stack([side, 1 - side])[None, :]).reshape(-1)

    weight_bytes = local_count * half_width * hidden * 2
    matmul_flops = 2 * local_count * slots * half_width * hidden
    hot_flops = local_count * slots * half_width * token_count
    groups = 4
    piece_sems, w_sems = copies((ep_count // PARTS,)), copies((groups,))
    rows_here = pltpu.VMEM((part_tokens, half_width), bf16)
    x_shape = jax.ShapeDtypeStruct((local_count, slots, half_width), bf16)
    x_here = pltpu.VMEM(x_shape.shape, bf16)
    w_here, down_here = pltpu.VMEM(w_gate.shape, bf16), pltpu.VMEM(w_down.shape, bf16)
    pre_shape = jax.ShapeDtypeStruct((local_count, slots, hidden), f32)
    half = local_count // HALVES
    part_of_pre = pltpu.HBM((half, slots, hidden), f32)
    pre_here = pltpu.VMEM(pre_shape.shape, f32)
    batch = 2 if local_count % 2 == 0 else 1

    def batched(*shape):
        return pl.BlockSpec((batch,) + shape, lambda e: (e, 0, 0))

    made = {}

    def beside_gather(turn, info, pieces):
        if turn == 1:
            (gate_w,) = tie([w_gate], *pieces)
            made["loaded"] = pl.pallas_call(
                load_kernel,
                out_shape=pltpu.VMEM(w_gate.shape, bf16),
                in_specs=[memory],
                out_specs=memory,
                scratch_shapes=[w_sems],
                compiler_params=params(24),
                cost_estimate=cost(0, weight_bytes),
                name="load",
            )(in_hbm(gate_w))
            return []
        made["slots"], made["gates"] = pl.pallas_call(
            functools.partial(route_kernel, top_count=top_count, block_rows=block_rows),
            out_shape=(
                jax.ShapeDtypeStruct((local_count, token_count), jnp.int32),
                jax.ShapeDtypeStruct((local_count, token_count), f32),
            ),
            in_specs=[smem, smem, vmem],
            out_specs=(vmem, vmem),
            compiler_params=params(16),
            cost_estimate=cost(1e7, 1e6),
            name="route",
        )(order, (place * local_count).reshape(1), info)
        part_shape = jax.ShapeDtypeStruct((local_count, part_slots, half_width), bf16)
        made["x"], made["grad_x"], made["slot_gates"] = pl.pallas_call(
            first_kernel,
            out_shape=(
                part_shape,
                part_shape,
                jax.ShapeDtypeStruct((local_count, slots, 128), f32),
            ),
            in_specs=[vmem] * 2 + [memory] * 4,
            out_specs=(vmem,) * 3,
            scratch_shapes=[rows_here, rows_here, piece_sems, piece_sems],
            compiler_params=params(32),
            cost_estimate=cost(hot_flops, weight_bytes / 2),
            name="first_slots",
        )(made["slots"], made["gates"], *pieces)
        return [made["x"], made["grad_x"]]

    pieces = gather_rows(jnp.stack([tokens, out_grad]), info, at_end, beside_gather)
    slot_of = made["slots"]

    x, *pre_parts = pl.pallas_call(
        pre_kernel,
        out_shape=(x_shape,) + (part_of_pre,) * (2 * HALVES),
        in_specs=[vmem] + [memory] * 5 + [vmem, memory],
        out_specs=(memory,) * (1 + 2 * HALVES),
        scratch_shapes=[rows_here, x_here, w_here, pre_here, pre_here]
        + [piece_sems, copies, w_sems, copies, w_sems, w_sems],
        compiler_params=params(24),
        cost_estimate=cost(hot_flops / 2 + 2 * matmul_flops, 2.8 * weight_bytes),
        name="pre",
    )(
        slot_of,
        *pieces[4:8],
        made["x"],
        in_vmem(made["loaded"]),
        in_hbm(w_up),
    )
    gate_parts, up_parts = pre_parts[:HALVES], pre_parts[HALVES:]
    grad_pieces = tie(pieces[8:], x)

    def down(start, pieces):
        return pl.pallas_call(
            functools.partial(down_kernel, start),
            out_shape=part_of_pre,
            in_specs=[vmem] + [memory] * 6,
            out_specs=memory,
            scratch_shapes=[
                rows_here,
                pltpu.VMEM((half, slots, half_width), bf16),
                pltpu.VMEM((half, hidden, half_width), bf16),
                pltpu.VMEM((half, slots, hidden), f32),
            ]
            + [piece_sems, copies, w_sems, w_sems],
            compiler_params=params(12),
            cost_estimate=cost((hot_flops / 2 + matmul_flops) / HALVES, 1.4 * weight_bytes / HALVES),
            name="down",
        )(slot_of, *pieces, made["grad_x"], in_hbm(w_down))

    piece_shape = jax.ShapeDtypeStruct((chunk, half_width), bf16)
    pieces_here = [pltpu.VMEM((LINES, chunk, half_width), bf16), copies((LINES,))]

    def rows(number, sources, before):
        scratch = [
            pltpu.VMEM((6, half, slots, hidden), f32),
            pltpu.VMEM((half, half_width, hidden), bf16),
            pltpu.VMEM((half, half_width, hidden), bf16),
            pltpu.VMEM((half, slots, 2 * hidden), bf16),
            pltpu.VMEM((PARTS, half * part_slots, half_width), bf16),
            copies((6, groups)),
            w_sems,
            w_sems,
            copies,
            copies,
        ]
        out_shape = [
            jax.ShapeDtypeStruct((half, slots, 2 * hidden), bf16),
            jax.ShapeDtypeStruct((half * part_slots, half_width), bf16),
        ]
        if before:
            out_shape += [piece_shape] * LINES
            out_specs = (memory,) * (2 + LINES)
            scratch += pieces_here
        else:
            out_shape += [pltpu.VMEM((part_tokens, half_width), f32)]
            out_specs = (memory, memory, vmem)
        return pl.pallas_call(
            functools.partial(rows_kernel, number * half),
            out_shape=tuple(out_shape),
            in_specs=[vmem] * 2 + [memory] * 8 + [vmem] * len(before),
            out_specs=out_specs,
            scratch_shapes=scratch,
            compiler_params=params(30),
            cost_estimate=cost(
                (2 * matmul_flops + hot_flops) / HALVES, 3.1 * weight_bytes / HALVES
            ),
            name="rows",
        )(slot_of, made["slot_gates"], *sources, in_hbm(w_gate), in_hbm(w_up), *before)

    def both(value):
        return [value, across_cores(value)]

    pre_first = [*both(gate_parts[0]), *both(up_parts[0])]
    raw_first = down(0, [*pieces[4:6], *grad_pieces])
    sent = both(raw_first)
    gate_last, up_last, *last_pieces = tie(
        [gate_parts[1], up_parts[1], *pieces[4:6], *grad_pieces], raw_first
    )
    pre_last = [*both(gate_last), *both(up_last)]
    raw_last = down(half, last_pieces)
    sent[1], pre_first[1], pre_first[3] = tie((sent[1], pre_first[1], pre_first[3]), raw_last)
    grads_first, near_first, sums = rows(0, [*pre_first, *sent], [])
    last = [*pre_last, *both(raw_last)]
    grads_last, near_last, *far_sums = rows(1, last, [in_vmem(sums)])
    grads = [grads_first, grads_last]
    near_first, near_last = tie((near_first, near_last), *far_sums)
    near_sums = pl.pallas_call(
        near_kernel,
        out_shape=(piece_shape,) * LINES,
        in_specs=[vmem] + [memory] * HALVES,
        out_specs=(memory,) * LINES,
        scratch_shapes=[
            pltpu.VMEM((local_count * part_slots, half_width), bf16),
            pieces_here[0],
            copies((HALVES,)),
            pieces_here[1],
        ],
        compiler_params=params(12),
        cost_estimate=cost(hot_flops / 2, weight_bytes / 3),
        name="near",
    )(slot_of, near_first, near_last)
    partial = [*near_sums, *far_sums]

    turns = LINES
    group = local_count // turns
    weight_shape = jax.ShapeDtypeStruct(w_gate.shape, bf16)
    weight_grads = []

    def block_of(first, *shape):
        return pl.BlockSpec((1,) + shape, lambda e: (first + e, 0, 0))

    def meanwhile(turn, values):
        first = turn * group
        operands = [x, grads[first // half]]
        operands = tie(operands, *(held or partial))
        weight_grads[:] = pl.pallas_call(
            weight_kernel,
            grid=(group,),
            out_shape=(weight_shape, weight_shape),
            in_specs=[block_of(first, slots, half_width), block_of(first % half, slots, 2 * hidden)]
            + [memory] * len(weight_grads),
            out_specs=(block_of(first, half_width, hidden), block_of(first, half_width, hidden)),
            input_output_aliases={2 + i: i for i in range(len(weight_grads))},
            compiler_params=params(32),
            cost_estimate=cost(2 * matmul_flops / turns, 2.5 * weight_bytes / turns),
            name="weight_grads",
        )(*operands, *weight_grads)
        *values, weight_grads[0], weight_grads[1] = tie([*values, *weight_grads])
        held[:] = values
        return values

    held = []
    grad_input = scatter_sums(partial, meanwhile)
    return (grad_input, *weight_grads)


def solution(mesh):
    in_specs = (
        P(("groups", "ep"), "dp"),
        P(("groups", "ep"), "dp"),
        P(("groups", "ep", "dp"), None),
        P(("groups", "ep", "dp"), None),
        P("ep", "dp", None),
        P("ep", "dp", None),
        P("ep", None, "dp"),
    )
    out_specs = (
        P(("groups", "ep"), "dp"),
        P(("groups", "ep"), "dp", None),
        P(("groups", "ep"), "dp", None),
    )
    ep_count = mesh.shape["ep"]
    body = gather_body if ep_count == 2 * LINES else exchange_body
    return jax.shard_map(body, mesh=mesh, in_specs=in_specs, out_specs=out_specs, check_vma=False)
```

```python
import functools

import jax
import jax.numpy as jnp
from jax import lax
from jax.experimental import pallas as pl
from jax.experimental.pallas import tpu as pltpu
from jax.sharding import PartitionSpec as P

CAP = 6


def route_slots(expert_ids, experts, stride, offset):
    flattened = expert_ids.reshape(-1)
    onehot = (flattened[:, None] == jnp.arange(experts, dtype=jnp.int32)[None, :]).astype(jnp.int32)
    ranking = jnp.sum(onehot * (jnp.cumsum(onehot, axis=0) - 1), axis=1)
    return flattened * stride + offset + ranking


def fill_slots(values, slot_ids, slot_count):
    zeroed = jnp.zeros((slot_count,) + values.shape[1:], values.dtype)
    return zeroed.at[slot_ids].set(values)


def swiglu_back(pre_gate, pre_up, raw_down, gate_rows):
    grad_hidden = gate_rows.astype(jnp.float32)[..., None] * raw_down
    sigmoid = jax.nn.sigmoid(pre_gate)
    grad_gate_pre = (grad_hidden * pre_up * sigmoid * (1.0 + pre_gate * (1.0 - sigmoid))).astype(
        jnp.bfloat16
    )
    grad_up_pre = (grad_hidden * pre_gate * sigmoid).astype(jnp.bfloat16)
    return (grad_gate_pre, grad_up_pre)


def share_pre_grads(grad_gate_pre, grad_up_pre):
    return (
        lax.all_gather(grad_gate_pre, "dp", axis=2, tiled=True),
        lax.all_gather(grad_up_pre, "dp", axis=2, tiled=True),
    )


def weight_terms(shaped_rows, both_gate, both_up):
    grad_gate_w = jnp.einsum(
        "nlbcd,nlbcf->ldf", shaped_rows, both_gate, preferred_element_type=jnp.float32
    )
    grad_up_w = jnp.einsum(
        "nlbcd,nlbcf->ldf", shaped_rows, both_up, preferred_element_type=jnp.float32
    )
    return (grad_gate_w.astype(jnp.bfloat16), grad_up_w.astype(jnp.bfloat16))


def expert_work(token_rows, grad_rows, gate_rows, w_gate, w_up, w_down):
    full_gate, full_up, full_down = (
        lax.all_gather(w_gate, "dp", axis=1, tiled=True),
        lax.all_gather(w_up, "dp", axis=1, tiled=True),
        lax.all_gather(w_down, "dp", axis=2, tiled=True),
    )
    pre_gate = jnp.einsum(
        "nlcd,ldf->nlcf", token_rows, full_gate, preferred_element_type=jnp.float32
    )
    pre_up = jnp.einsum("nlcd,ldf->nlcf", token_rows, full_up, preferred_element_type=jnp.float32)
    raw_down = jnp.einsum(
        "nlcd,lfd->nlcf", grad_rows, full_down, preferred_element_type=jnp.float32
    )
    grad_gate_pre, grad_up_pre = swiglu_back(pre_gate, pre_up, raw_down, gate_rows)
    row_grad = (
        jnp.einsum("nlcf,ldf->nlcd", grad_gate_pre, full_gate, preferred_element_type=jnp.float32)
        + jnp.einsum("nlcf,ldf->nlcd", grad_up_pre, full_up, preferred_element_type=jnp.float32)
    ).astype(jnp.bfloat16)
    return (row_grad, grad_gate_pre, grad_up_pre)


def exchange_body(tokens, out_grad, route_gates, expert_ids, w_gate, w_up, w_down):
    ep_count = lax.axis_size("ep")
    local_count = w_gate.shape[0]
    experts = local_count * ep_count
    block_rows, top_count = expert_ids.shape
    capacity = CAP
    half_width = tokens.shape[1]
    feature_width = 2 * half_width
    pair_ids = lax.all_gather(expert_ids, "dp", axis=0, tiled=True)
    first_slots = route_slots(pair_ids[:block_rows], experts, 2 * capacity, 0)
    second_slots = route_slots(pair_ids[block_rows:], experts, 2 * capacity, capacity)
    slot_ids = jnp.concatenate([first_slots, second_slots])
    own_slots = lax.dynamic_index_in_dim(
        slot_ids.reshape(2, block_rows * top_count), lax.axis_index("dp"), 0, keepdims=False
    )
    token_of = jnp.arange(2 * block_rows * top_count, dtype=jnp.int32) // top_count
    slot_count = experts * 2 * capacity
    send_rows = fill_slots(tokens[token_of], slot_ids, slot_count).reshape(
        ep_count, local_count * 2 * capacity, half_width
    )
    send_grads = fill_slots(out_grad[token_of], slot_ids, slot_count).reshape(
        ep_count, local_count * 2 * capacity, half_width
    )
    send_gates = fill_slots(route_gates.reshape(-1), own_slots, slot_count).reshape(
        ep_count, local_count * 2 * capacity
    )
    recv_rows, recv_grads, recv_gates = (
        lax.all_to_all(send_rows, "ep", split_axis=0, concat_axis=0, tiled=True),
        lax.all_to_all(send_grads, "ep", split_axis=0, concat_axis=0, tiled=True),
        lax.all_to_all(send_gates, "ep", split_axis=0, concat_axis=0, tiled=True),
    )
    shaped_rows = recv_rows.reshape(ep_count, local_count, 2, capacity, half_width)
    shaped_grads = recv_grads.reshape(ep_count, local_count, 2, capacity, half_width)
    shaped_gates = recv_gates.reshape(ep_count, local_count, 2, capacity)
    joined_rows, joined_grads = (
        lax.all_to_all(shaped_rows, "dp", split_axis=2, concat_axis=4, tiled=True),
        lax.all_to_all(shaped_grads, "dp", split_axis=2, concat_axis=4, tiled=True),
    )
    token_rows = joined_rows.reshape(ep_count, local_count, capacity, feature_width)
    grad_rows = joined_grads.reshape(ep_count, local_count, capacity, feature_width)
    gate_rows = lax.dynamic_index_in_dim(shaped_gates, lax.axis_index("dp"), 2, keepdims=False)
    row_grad, grad_gate_pre, grad_up_pre = expert_work(
        token_rows, grad_rows, gate_rows, w_gate, w_up, w_down
    )
    both_gate, both_up = share_pre_grads(
        grad_gate_pre.reshape(ep_count, local_count, 1, capacity, -1),
        grad_up_pre.reshape(ep_count, local_count, 1, capacity, -1),
    )
    spread = lax.all_to_all(
        row_grad.reshape(ep_count, local_count, 1, capacity, feature_width),
        "dp",
        split_axis=4,
        concat_axis=2,
        tiled=True,
    )
    grad_gate_w, grad_up_w = weight_terms(shaped_rows, both_gate, both_up)
    returned = lax.all_to_all(
        spread.reshape(ep_count, local_count * 2 * capacity, half_width),
        "ep",
        split_axis=0,
        concat_axis=0,
        tiled=True,
    )
    returned = returned.reshape(slot_count, half_width)
    per_route = (
        returned[slot_ids].astype(jnp.float32).reshape(2 * block_rows, top_count, half_width)
    )
    grad_input = jnp.sum(per_route, axis=1).astype(jnp.bfloat16)
    return (grad_input, grad_gate_w, grad_up_w)


ORDERS = ((0, 1, 2, 3), (1, 0, 2, 3), (2, 3, 1, 0), (3, 2, 1, 0))
LINES = len(ORDERS)
PARTS = 2
HALVES = 2
OUTER = ((0, 1), (1, 0), (2, 3), (3, 2))
INNER = ((1, 2), (2, 1))
TO_END = ((1, 0), (2, 3))
FROM_END = ((0, 1), (3, 2))


def along_line(value, moves):
    pairs = [(2 * a + side, 2 * b + side) for a, b in moves for side in range(2)]
    return lax.ppermute(value, "ep", pairs)


def across_pair(value):
    return lax.ppermute(value, "ep", [(i, i ^ 1) for i in range(2 * LINES)])


def across_cores(value):
    return lax.ppermute(value, "dp", [(0, 1), (1, 0)])


def tie(values, *others):
    values = list(values)
    return list(lax.optimization_barrier(tuple(values) + tuple(others))[: len(values)])


def gather_rows(rows, info, at_end, meanwhile):
    def widen(info, bits):
        came = [
            lax.ppermute(info, "ep", [(i, i ^ bit) for i in range(2 * LINES)]) for bit in bits
        ]
        return functools.reduce(jnp.add, came, info)

    outer, inner, other = along_line(rows, OUTER), along_line(rows, INNER), across_pair(rows)
    info = widen(info + across_cores(info), [1])
    info = widen(info, [2])
    outer, inner, other, info = tie((outer, inner, other, info))
    pieces = [rows, other]

    second, third = along_line(inner, TO_END), along_line(outer, INNER)
    other = across_pair(outer)
    info = widen(info, [4])
    second, third, other = tie((second, third, other))
    pieces += [outer, other]

    middle = jnp.where(at_end, second, inner)
    last, other = along_line(third, TO_END), across_pair(middle)
    done = meanwhile(0, info, pieces)
    last, other = tie((last, other), *done)
    pieces += [middle, other]

    meanwhile(1, info, [last, other])
    for part in range(2):
        far = jnp.where(at_end, last[part], third[part])
        pieces += [far, across_pair(far)]
        last, third = tie((last, third))
    return pieces


def scatter_sums(partial, meanwhile):
    f32, bf16 = jnp.float32, jnp.bfloat16

    def own_side(m, other):
        return partial[2 * m].astype(f32) + other.astype(f32)

    other = across_pair(partial[7])
    (other,) = meanwhile(0, [other])
    far = own_side(3, other)
    outward, other = along_line(far.astype(bf16), FROM_END), across_pair(partial[5])
    outward, other = meanwhile(1, [outward, other])
    middle = own_side(2, other)
    crossed = along_line((far + outward.astype(f32)).astype(bf16), INNER)
    outward, other = along_line(middle.astype(bf16), FROM_END), across_pair(partial[3])
    crossed, outward, other = meanwhile(2, [crossed, outward, other])
    near = own_side(1, other) + crossed.astype(f32)
    inner = along_line((middle + outward.astype(f32)).astype(bf16), INNER)
    outer, other = along_line(near.astype(bf16), OUTER), across_pair(partial[1])
    inner, outer, other = meanwhile(3, [inner, outer, other])
    total = own_side(0, other) + outer.astype(f32) + inner.astype(f32)
    return total.astype(bf16)


def route_kernel(order_ref, base_ref, info_ref, slot_ref, gate_ref, *, top_count, block_rows):
    local_count = slot_ref.shape[0]
    chunk = info_ref.shape[2]
    row = lax.broadcasted_iota(jnp.int32, (chunk, chunk), 0)
    column = lax.broadcasted_iota(jnp.int32, (chunk, chunk), 1)
    before = ((row < column) & (row // block_rows == column // block_rows)).astype(jnp.bfloat16)
    lane = lax.broadcasted_iota(jnp.int32, (local_count, chunk), 1)
    expert = (base_ref[0] + lax.broadcasted_iota(jnp.int32, (local_count, chunk), 0)).astype(
        jnp.float32
    )
    for piece in range(info_ref.shape[0]):
        info = info_ref[order_ref[piece]].astype(jnp.float32)
        named = jnp.zeros((local_count, chunk), jnp.float32)
        gate = jnp.zeros((local_count, chunk), jnp.float32)
        for k in range(top_count):
            match = info[k : k + 1, :] == expert
            named = jnp.where(match, 1.0, named)
            gate = jnp.where(match, info[top_count + k : top_count + k + 1, :], gate)
        rank = jnp.dot(
            named.astype(jnp.bfloat16), before, preferred_element_type=jnp.float32
        ).astype(jnp.int32)
        block = piece * (chunk // block_rows) + lane // block_rows
        columns = pl.ds(piece * chunk, chunk)
        slot_ref[:, columns] = jnp.where(named > 0.5, block * CAP + rank, -1)
        gate_ref[:, columns] = gate


def start_all(copies):
    for copy in copies:
        copy.start()
    return copies


def piece_copies(sources, rows_ref, sems):
    chunk = rows_ref.shape[0] // len(sources)
    return start_all(
        [
            pltpu.make_async_copy(source, rows_ref.at[pl.ds(m * chunk, chunk)], sems.at[m])
            for m, source in enumerate(sources)
        ]
    )


def group_copies(source, target, sems):
    count, number = target.shape[0], sems.shape[0]
    group = count // number
    return start_all(
        [
            pltpu.make_async_copy(
                source.at[pl.ds(i * group, group)], target.at[pl.ds(i * group, group)], sems.at[i]
            )
            for i in range(number)
        ]
    )


def hot_part(slot_ref, experts, part, slots):
    tokens = slot_ref.shape[1] // PARTS
    count = slots // PARTS
    columns = slice(part * tokens, (part + 1) * tokens)
    row = lax.broadcasted_iota(jnp.int32, (count, tokens), 0) + part * count
    return [row == slot_ref[e : e + 1, columns] for e in experts]


def dispatch(part, slot_ref, rows_ref, x_ref, start=0):
    local_count = x_ref.shape[0]
    count = 2 * LINES * 2 * CAP // PARTS
    first_slot = part * count if x_ref.shape[1] > count else 0
    group = min(8, local_count)
    for first in range(0, local_count, group):
        experts = range(start + first, start + first + group)
        hot = jnp.concatenate(
            [h.astype(jnp.bfloat16) for h in hot_part(slot_ref, experts, part, count * PARTS)]
        )
        found = jnp.dot(hot, rows_ref[...], preferred_element_type=jnp.float32)
        found = found.astype(jnp.bfloat16)
        for i, e in enumerate(experts):
            x_ref[e - start, first_slot : first_slot + count] = found[i * count : (i + 1) * count]


def first_kernel(slot_ref, gates_ref, *refs):
    pieces, (x_ref, grad_x_ref, slot_gates_ref) = refs[:4], refs[4:7]
    tokens_here, grads_here, token_sems, grad_sems = refs[7:]
    tokens = piece_copies([piece.at[0] for piece in pieces], tokens_here, token_sems)
    grads = piece_copies([piece.at[1] for piece in pieces], grads_here, grad_sems)
    for arrivals, rows_ref, target in (
        (tokens, tokens_here, x_ref),
        (grads, grads_here, grad_x_ref),
    ):
        for copy in arrivals:
            copy.wait()
        dispatch(0, slot_ref, rows_ref, target)
    local_count, slots, lanes = slot_gates_ref.shape
    tokens, count = slot_ref.shape[1] // PARTS, slots // PARTS
    for e in range(local_count):
        for part in range(PARTS):
            gates = gates_ref[e : e + 1, part * tokens : (part + 1) * tokens]
            gate = jnp.where(hot_part(slot_ref, [e], part, slots)[0], gates, 0.0)
            slot_gates_ref[e, part * count : (part + 1) * count] = jnp.broadcast_to(
                jnp.sum(gate, axis=1, keepdims=True), (count, lanes)
            )


def finish_slots(
    index, slot_ref, pieces, first_ref, rows_ref, x_here, piece_sems, first_sem, start=0
):
    sources = [piece.at[index] if len(piece.shape) == 3 else piece for piece in pieces]
    arrivals = piece_copies(sources, rows_ref, piece_sems)
    experts = pl.ds(start, x_here.shape[0])
    first = pltpu.make_async_copy(
        first_ref.at[experts], x_here.at[:, pl.ds(0, first_ref.shape[1])], first_sem
    )
    first.start()

    def finish():
        for copy in arrivals:
            copy.wait()
        dispatch(1, slot_ref, rows_ref, x_here, start)
        first.wait()

    return finish


def multiply(x_ref, w_ref, here, out_refs, out_sems, weights=None, side=0):
    groups = out_sems.shape[0]
    group = x_ref.shape[0] // groups
    copies = []
    for i in range(groups):
        if weights is not None:
            weights[i].wait()
        for e in range(i * group, (i + 1) * group):
            here[e] = lax.dot_general(
                x_ref[e],
                w_ref[e],
                (((1,), (side,)), ((), ())),
                preferred_element_type=jnp.float32,
            )
        span, each = pl.ds(i * group, group), groups // len(out_refs)
        target = out_refs[i // each].at[pl.ds(i % each * group, group)]
        copies += start_all([pltpu.make_async_copy(here.at[span], target, out_sems.at[i])])
    return copies


def load_kernel(w_ref, out_ref, sems):
    for copy in group_copies(w_ref, out_ref, sems):
        copy.wait()


def pre_kernel(slot_ref, *refs):
    pieces, refs = refs[:4], refs[4:]
    first_ref, gate_w, up_w, x_ref = refs[:4]
    gate_refs, up_refs = refs[4 : 4 + HALVES], refs[4 + HALVES : 4 + 2 * HALVES]
    refs = refs[4 + 2 * HALVES :]
    rows_here, x_here, up_w_here, gate_here, up_here = refs[:5]
    piece_sems, first_sem, up_w_sems, x_sem, gate_sems, up_sems = refs[5:]
    finish = finish_slots(
        0, slot_ref, pieces, first_ref, rows_here, x_here, piece_sems, first_sem
    )
    up_ws = group_copies(up_w, up_w_here, up_w_sems)
    finish()
    copies = start_all([pltpu.make_async_copy(x_here, x_ref, x_sem)])
    copies += multiply(x_here, gate_w, gate_here, gate_refs, gate_sems)
    copies += multiply(x_here, up_w_here, up_here, up_refs, up_sems, up_ws)
    for copy in copies:
        copy.wait()


def down_kernel(start, slot_ref, *refs):
    pieces, refs = refs[:4], refs[4:]
    first_ref, down_w, raw_ref = refs[:3]
    rows_here, x_here, w_here, here, piece_sems, first_sem, w_sems, out_sems = refs[3:]
    finish = finish_slots(
        1, slot_ref, pieces, first_ref, rows_here, x_here, piece_sems, first_sem, start
    )
    weights = group_copies(down_w.at[pl.ds(start, x_here.shape[0])], w_here, w_sems)
    finish()
    for copy in multiply(x_here, w_here, here, [raw_ref], out_sems, weights, 1):
        copy.wait()


def keep_row(row, e, rows_ref):
    count = row.shape[0] // PARTS
    for part in range(PARTS):
        rows_ref[part, e * count : (e + 1) * count] = row[part * count : (part + 1) * count]


def sum_rows(part, start, local_count, slot_ref, rows, slots):
    experts = range(start, start + local_count)
    hot = jnp.concatenate(
        [h.astype(jnp.bfloat16) for h in hot_part(slot_ref, experts, part, slots)]
    )
    return lax.dot_general(
        hot, rows, (((0,), (0,)), ((), ())), preferred_element_type=jnp.float32
    )


def give_out(total, outs_here, out_refs, out_sems):
    rows = total.shape[0] // len(out_refs)
    for i in range(len(out_refs)):
        outs_here[i] = total[i * rows : (i + 1) * rows].astype(jnp.bfloat16)
    return start_all(
        [
            pltpu.make_async_copy(outs_here.at[i], out_ref, out_sems.at[i])
            for i, out_ref in enumerate(out_refs)
        ]
    )


def rows_kernel(start, slot_ref, slot_gates_ref, *refs):
    sources, gate_w, up_w, refs = refs[:6], refs[6], refs[7], refs[8:]
    last = start > 0
    if last:
        before_ref, refs = refs[0], refs[1:]
    grads_ref, near_ref, refs = refs[0], refs[1], refs[2:]
    if last:
        out_refs, refs = refs[:LINES], refs[LINES:]
        outs_here, out_sems = refs[-2:]
    else:
        sum_ref, refs = refs[0], refs[1:]
    inputs_here, gate_here, up_here, grads_here, rows_ref = refs[:5]
    input_sems, gate_sems, up_sems, grads_sem, near_sem = refs[5:10]
    local_count, slots, hidden = inputs_here.shape[1:]
    groups = input_sems.shape[1]
    group = local_count // groups
    arrivals = []
    for i in range(groups):
        here, there = pl.ds(i * group, group), pl.ds(start + i * group, group)
        moves = [
            pltpu.make_async_copy(source.at[here], inputs_here.at[j, here], input_sems.at[j, i])
            for j, source in enumerate(sources)
        ]
        moves += [
            pltpu.make_async_copy(gate_w.at[there], gate_here.at[here], gate_sems.at[i]),
            pltpu.make_async_copy(up_w.at[there], up_here.at[here], up_sems.at[i]),
        ]
        arrivals.append(start_all(moves))
    for i in range(groups):
        for copy in arrivals[i]:
            copy.wait()
        for e in range(i * group, (i + 1) * group):
            pre_gate = inputs_here[0, e] + inputs_here[1, e]
            pre_up = inputs_here[2, e] + inputs_here[3, e]
            raw = inputs_here[4, e] + inputs_here[5, e]
            sigmoid = jax.nn.sigmoid(pre_gate)
            scaled = slot_gates_ref[start + e, :, :1] * raw * sigmoid
            grad_gate = (scaled * pre_up * (1.0 + pre_gate * (1.0 - sigmoid))).astype(jnp.bfloat16)
            grad_up = (scaled * pre_gate).astype(jnp.bfloat16)
            grads_here[e, :, :hidden] = grad_gate
            grads_here[e, :, hidden:] = grad_up
            turned = (((1,), (1,)), ((), ()))
            row = lax.dot_general(
                grad_gate, gate_here[e], turned, preferred_element_type=jnp.float32
            )
            row += lax.dot_general(grad_up, up_here[e], turned, preferred_element_type=jnp.float32)
            keep_row(row.astype(jnp.bfloat16), e, rows_ref)
    copies = start_all(
        [
            pltpu.make_async_copy(grads_here, grads_ref, grads_sem),
            pltpu.make_async_copy(rows_ref.at[0], near_ref, near_sem),
        ]
    )
    total = sum_rows(1, start, local_count, slot_ref, rows_ref[1], slots)
    if last:
        copies += give_out(total + before_ref[...], outs_here, out_refs, out_sems)
    else:
        sum_ref[...] = total
    for copy in copies:
        copy.wait()


def near_kernel(slot_ref, *refs):
    rows_refs, out_refs = refs[:HALVES], refs[HALVES : HALVES + LINES]
    rows_here, outs_here, row_sems, out_sems = refs[HALVES + LINES :]
    count = rows_here.shape[0] // HALVES
    copies = start_all(
        [
            pltpu.make_async_copy(ref, rows_here.at[pl.ds(i * count, count)], row_sems.at[i])
            for i, ref in enumerate(rows_refs)
        ]
    )
    for copy in copies:
        copy.wait()
    local_count = slot_ref.shape[0]
    slots = PARTS * rows_here.shape[0] // local_count
    total = sum_rows(0, 0, local_count, slot_ref, rows_here[...], slots)
    for copy in give_out(total, outs_here, out_refs, out_sems):
        copy.wait()


def weight_kernel(x_ref, grads_ref, *refs):
    gate_out_ref, up_out_ref = refs[-2:]
    hidden = gate_out_ref.shape[-1]
    for i in range(x_ref.shape[0]):
        found = lax.dot_general(
            x_ref[i], grads_ref[i], (((0,), (0,)), ((), ())), preferred_element_type=jnp.float32
        ).astype(jnp.bfloat16)
        gate_out_ref[i] = found[:, :hidden]
        up_out_ref[i] = found[:, hidden:]


def in_hbm(value):
    return pltpu.with_memory_space_constraint(value, pltpu.HBM)


def in_vmem(value):
    return pltpu.with_memory_space_constraint(value, pltpu.VMEM)


def params(mib):
    return pltpu.CompilerParams(vmem_limit_bytes=mib * 1024 * 1024)


def cost(flops, moved):
    return pl.CostEstimate(flops=int(flops), bytes_accessed=int(moved), transcendentals=0)


def gather_body(tokens, out_grad, route_gates, expert_ids, w_gate, w_up, w_down):
    ep_count = 2 * LINES
    local_count, half_width, hidden = w_gate.shape
    block_rows, top_count = expert_ids.shape
    chunk = 2 * block_rows
    token_count = ep_count * chunk
    slots = 2 * ep_count * CAP
    part_slots, part_tokens = slots // PARTS, token_count // PARTS
    place = lax.axis_index("ep")
    here, side = place // 2, place % 2
    at_end = (here == 0) | (here == LINES - 1)
    bf16, f32 = jnp.bfloat16, jnp.float32
    memory = pl.BlockSpec(memory_space=pl.ANY)
    smem = pl.BlockSpec(memory_space=pltpu.SMEM)
    vmem = pl.BlockSpec(memory_space=pltpu.VMEM)
    copies = pltpu.SemaphoreType.DMA

    own_info = jnp.concatenate([expert_ids.astype(bf16), route_gates], axis=1).T
    info = jnp.zeros((ep_count, 2 * top_count, chunk), bf16)
    info = lax.dynamic_update_slice(
        info, own_info[None], (place, 0, lax.axis_index("dp") * block_rows)
    )
    line_order = jnp.asarray(ORDERS, jnp.int32)[here]
    order = (2 * line_order[:, None] + jnp.stack([side, 1 - side])[None, :]).reshape(-1)

    weight_bytes = local_count * half_width * hidden * 2
    matmul_flops = 2 * local_count * slots * half_width * hidden
    hot_flops = local_count * slots * half_width * token_count
    groups = 4
    piece_sems, w_sems = copies((ep_count // PARTS,)), copies((groups,))
    rows_here = pltpu.VMEM((part_tokens, half_width), bf16)
    x_shape = jax.ShapeDtypeStruct((local_count, slots, half_width), bf16)
    x_here = pltpu.VMEM(x_shape.shape, bf16)
    w_here, down_here = pltpu.VMEM(w_gate.shape, bf16), pltpu.VMEM(w_down.shape, bf16)
    pre_shape = jax.ShapeDtypeStruct((local_count, slots, hidden), f32)
    half = local_count // HALVES
    part_of_pre = pltpu.HBM((half, slots, hidden), f32)
    pre_here = pltpu.VMEM(pre_shape.shape, f32)
    batch = 2 if local_count % 2 == 0 else 1

    def batched(*shape):
        return pl.BlockSpec((batch,) + shape, lambda e: (e, 0, 0))

    made = {}

    def beside_gather(turn, info, pieces):
        if turn == 1:
            (gate_w,) = tie([w_gate], *pieces)
            made["loaded"] = pl.pallas_call(
                load_kernel,
                out_shape=pltpu.VMEM(w_gate.shape, bf16),
                in_specs=[memory],
                out_specs=memory,
                scratch_shapes=[w_sems],
                compiler_params=params(24),
                cost_estimate=cost(0, weight_bytes),
                name="load",
            )(in_hbm(gate_w))
            return []
        made["slots"], made["gates"] = pl.pallas_call(
            functools.partial(route_kernel, top_count=top_count, block_rows=block_rows),
            out_shape=(
                jax.ShapeDtypeStruct((local_count, token_count), jnp.int32),
                jax.ShapeDtypeStruct((local_count, token_count), f32),
            ),
            in_specs=[smem, smem, vmem],
            out_specs=(vmem, vmem),
            compiler_params=params(16),
            cost_estimate=cost(1e7, 1e6),
            name="route",
        )(order, (place * local_count).reshape(1), info)
        part_shape = jax.ShapeDtypeStruct((local_count, part_slots, half_width), bf16)
        made["x"], made["grad_x"], made["slot_gates"] = pl.pallas_call(
            first_kernel,
            out_shape=(
                part_shape,
                part_shape,
                jax.ShapeDtypeStruct((local_count, slots, 128), f32),
            ),
            in_specs=[vmem] * 2 + [memory] * 4,
            out_specs=(vmem,) * 3,
            scratch_shapes=[rows_here, rows_here, piece_sems, piece_sems],
            compiler_params=params(32),
            cost_estimate=cost(hot_flops, weight_bytes / 2),
            name="first_slots",
        )(made["slots"], made["gates"], *pieces)
        return [made["x"], made["grad_x"]]

    pieces = gather_rows(jnp.stack([tokens, out_grad]), info, at_end, beside_gather)
    slot_of = made["slots"]

    x, *pre_parts = pl.pallas_call(
        pre_kernel,
        out_shape=(x_shape,) + (part_of_pre,) * (2 * HALVES),
        in_specs=[vmem] + [memory] * 5 + [vmem, memory],
        out_specs=(memory,) * (1 + 2 * HALVES),
        scratch_shapes=[rows_here, x_here, w_here, pre_here, pre_here]
        + [piece_sems, copies, w_sems, copies, w_sems, w_sems],
        compiler_params=params(24),
        cost_estimate=cost(hot_flops / 2 + 2 * matmul_flops, 2.8 * weight_bytes),
        name="pre",
    )(
        slot_of,
        *pieces[4:8],
        made["x"],
        in_vmem(made["loaded"]),
        in_hbm(w_up),
    )
    gate_parts, up_parts = pre_parts[:HALVES], pre_parts[HALVES:]
    grad_pieces = tie(pieces[8:], x)

    def down(start, pieces):
        return pl.pallas_call(
            functools.partial(down_kernel, start),
            out_shape=part_of_pre,
            in_specs=[vmem] + [memory] * 6,
            out_specs=memory,
            scratch_shapes=[
                rows_here,
                pltpu.VMEM((half, slots, half_width), bf16),
                pltpu.VMEM((half, hidden, half_width), bf16),
                pltpu.VMEM((half, slots, hidden), f32),
            ]
            + [piece_sems, copies, w_sems, w_sems],
            compiler_params=params(12),
            cost_estimate=cost((hot_flops / 2 + matmul_flops) / HALVES, 1.4 * weight_bytes / HALVES),
            name="down",
        )(slot_of, *pieces, made["grad_x"], in_hbm(w_down))

    piece_shape = jax.ShapeDtypeStruct((chunk, half_width), bf16)
    pieces_here = [pltpu.VMEM((LINES, chunk, half_width), bf16), copies((LINES,))]

    def rows(number, sources, before):
        scratch = [
            pltpu.VMEM((6, half, slots, hidden), f32),
            pltpu.VMEM((half, half_width, hidden), bf16),
            pltpu.VMEM((half, half_width, hidden), bf16),
            pltpu.VMEM((half, slots, 2 * hidden), bf16),
            pltpu.VMEM((PARTS, half * part_slots, half_width), bf16),
            copies((6, groups)),
            w_sems,
            w_sems,
            copies,
            copies,
        ]
        out_shape = [
            jax.ShapeDtypeStruct((half, slots, 2 * hidden), bf16),
            jax.ShapeDtypeStruct((half * part_slots, half_width), bf16),
        ]
        if before:
            out_shape += [piece_shape] * LINES
            out_specs = (memory,) * (2 + LINES)
            scratch += pieces_here
        else:
            out_shape += [pltpu.VMEM((part_tokens, half_width), f32)]
            out_specs = (memory, memory, vmem)
        return pl.pallas_call(
            functools.partial(rows_kernel, number * half),
            out_shape=tuple(out_shape),
            in_specs=[vmem] * 2 + [memory] * 8 + [vmem] * len(before),
            out_specs=out_specs,
            scratch_shapes=scratch,
            compiler_params=params(30),
            cost_estimate=cost(
                (2 * matmul_flops + hot_flops) / HALVES, 3.1 * weight_bytes / HALVES
            ),
            name="rows",
        )(slot_of, made["slot_gates"], *sources, in_hbm(w_gate), in_hbm(w_up), *before)

    def both(value):
        return [value, across_cores(value)]

    pre_first = [*both(gate_parts[0]), *both(up_parts[0])]
    raw_first = down(0, [*pieces[4:6], *grad_pieces])
    sent = both(raw_first)
    gate_last, up_last, *last_pieces = tie(
        [gate_parts[1], up_parts[1], *pieces[4:6], *grad_pieces], raw_first
    )
    pre_last = [*both(gate_last), *both(up_last)]
    raw_last = down(half, last_pieces)
    sent[1], pre_first[1], pre_first[3] = tie((sent[1], pre_first[1], pre_first[3]), raw_last)
    grads_first, near_first, sums = rows(0, [*pre_first, *sent], [])
    last = [*pre_last, *both(raw_last)]
    grads_last, near_last, *far_sums = rows(1, last, [in_vmem(sums)])
    grads = [grads_first, grads_last]
    near_first, near_last = tie((near_first, near_last), *far_sums)
    near_sums = pl.pallas_call(
        near_kernel,
        out_shape=(piece_shape,) * LINES,
        in_specs=[vmem] + [memory] * HALVES,
        out_specs=(memory,) * LINES,
        scratch_shapes=[
            pltpu.VMEM((local_count * part_slots, half_width), bf16),
            pieces_here[0],
            copies((HALVES,)),
            pieces_here[1],
        ],
        compiler_params=params(12),
        cost_estimate=cost(hot_flops / 2, weight_bytes / 3),
        name="near",
    )(slot_of, near_first, near_last)
    partial = [*near_sums, *far_sums]

    turns = LINES
    group = local_count // turns
    weight_shape = jax.ShapeDtypeStruct(w_gate.shape, bf16)
    weight_grads = []

    def block_of(first, *shape):
        return pl.BlockSpec((1,) + shape, lambda e: (first + e, 0, 0))

    def meanwhile(turn, values):
        first = turn * group
        operands = [x, grads[first // half]]
        operands = tie(operands, *(held or partial))
        weight_grads[:] = pl.pallas_call(
            weight_kernel,
            grid=(group,),
            out_shape=(weight_shape, weight_shape),
            in_specs=[block_of(first, slots, half_width), block_of(first % half, slots, 2 * hidden)]
            + [memory] * len(weight_grads),
            out_specs=(block_of(first, half_width, hidden), block_of(first, half_width, hidden)),
            input_output_aliases={2 + i: i for i in range(len(weight_grads))},
            compiler_params=params(32),
            cost_estimate=cost(2 * matmul_flops / turns, 2.5 * weight_bytes / turns),
            name="weight_grads",
        )(*operands, *weight_grads)
        *values, weight_grads[0], weight_grads[1] = tie([*values, *weight_grads])
        held[:] = values
        return values

    held = []
    grad_input = scatter_sums(partial, meanwhile)
    return (grad_input, *weight_grads)


def solution(mesh):
    in_specs = (
        P(("groups", "ep"), "dp"),
        P(("groups", "ep"), "dp"),
        P(("groups", "ep", "dp"), None),
        P(("groups", "ep", "dp"), None),
        P("ep", "dp", None),
        P("ep", "dp", None),
        P("ep", None, "dp"),
    )
    out_specs = (
        P(("groups", "ep"), "dp"),
        P(("groups", "ep"), "dp", None),
        P(("groups", "ep"), "dp", None),
    )
    ep_count = mesh.shape["ep"]
    body = gather_body if ep_count == 2 * LINES else exchange_body
    return jax.shard_map(body, mesh=mesh, in_specs=in_specs, out_specs=out_specs, check_vma=False)
```

```python
import functools

import jax
import jax.numpy as jnp
from jax import lax
from jax.experimental import pallas as pl
from jax.experimental.pallas import tpu as pltpu
from jax.sharding import PartitionSpec as P

CAP = 6


def route_slots(expert_ids, experts, stride, offset):
    flattened = expert_ids.reshape(-1)
    onehot = (flattened[:, None] == jnp.arange(experts, dtype=jnp.int32)[None, :]).astype(jnp.int32)
    ranking = jnp.sum(onehot * (jnp.cumsum(onehot, axis=0) - 1), axis=1)
    return flattened * stride + offset + ranking


def fill_slots(values, slot_ids, slot_count):
    zeroed = jnp.zeros((slot_count,) + values.shape[1:], values.dtype)
    return zeroed.at[slot_ids].set(values)


def swiglu_back(pre_gate, pre_up, raw_down, gate_rows):
    grad_hidden = gate_rows.astype(jnp.float32)[..., None] * raw_down
    sigmoid = jax.nn.sigmoid(pre_gate)
    grad_gate_pre = (grad_hidden * pre_up * sigmoid * (1.0 + pre_gate * (1.0 - sigmoid))).astype(
        jnp.bfloat16
    )
    grad_up_pre = (grad_hidden * pre_gate * sigmoid).astype(jnp.bfloat16)
    return (grad_gate_pre, grad_up_pre)


def share_pre_grads(grad_gate_pre, grad_up_pre):
    return (
        lax.all_gather(grad_gate_pre, "dp", axis=2, tiled=True),
        lax.all_gather(grad_up_pre, "dp", axis=2, tiled=True),
    )


def weight_terms(shaped_rows, both_gate, both_up):
    grad_gate_w = jnp.einsum(
        "nlbcd,nlbcf->ldf", shaped_rows, both_gate, preferred_element_type=jnp.float32
    )
    grad_up_w = jnp.einsum(
        "nlbcd,nlbcf->ldf", shaped_rows, both_up, preferred_element_type=jnp.float32
    )
    return (grad_gate_w.astype(jnp.bfloat16), grad_up_w.astype(jnp.bfloat16))


def expert_work(token_rows, grad_rows, gate_rows, w_gate, w_up, w_down):
    full_gate, full_up, full_down = (
        lax.all_gather(w_gate, "dp", axis=1, tiled=True),
        lax.all_gather(w_up, "dp", axis=1, tiled=True),
        lax.all_gather(w_down, "dp", axis=2, tiled=True),
    )
    pre_gate = jnp.einsum(
        "nlcd,ldf->nlcf", token_rows, full_gate, preferred_element_type=jnp.float32
    )
    pre_up = jnp.einsum("nlcd,ldf->nlcf", token_rows, full_up, preferred_element_type=jnp.float32)
    raw_down = jnp.einsum(
        "nlcd,lfd->nlcf", grad_rows, full_down, preferred_element_type=jnp.float32
    )
    grad_gate_pre, grad_up_pre = swiglu_back(pre_gate, pre_up, raw_down, gate_rows)
    row_grad = (
        jnp.einsum("nlcf,ldf->nlcd", grad_gate_pre, full_gate, preferred_element_type=jnp.float32)
        + jnp.einsum("nlcf,ldf->nlcd", grad_up_pre, full_up, preferred_element_type=jnp.float32)
    ).astype(jnp.bfloat16)
    return (row_grad, grad_gate_pre, grad_up_pre)


def exchange_body(tokens, out_grad, route_gates, expert_ids, w_gate, w_up, w_down):
    ep_count = lax.axis_size("ep")
    local_count = w_gate.shape[0]
    experts = local_count * ep_count
    block_rows, top_count = expert_ids.shape
    capacity = CAP
    half_width = tokens.shape[1]
    feature_width = 2 * half_width
    pair_ids = lax.all_gather(expert_ids, "dp", axis=0, tiled=True)
    first_slots = route_slots(pair_ids[:block_rows], experts, 2 * capacity, 0)
    second_slots = route_slots(pair_ids[block_rows:], experts, 2 * capacity, capacity)
    slot_ids = jnp.concatenate([first_slots, second_slots])
    own_slots = lax.dynamic_index_in_dim(
        slot_ids.reshape(2, block_rows * top_count), lax.axis_index("dp"), 0, keepdims=False
    )
    token_of = jnp.arange(2 * block_rows * top_count, dtype=jnp.int32) // top_count
    slot_count = experts * 2 * capacity
    send_rows = fill_slots(tokens[token_of], slot_ids, slot_count).reshape(
        ep_count, local_count * 2 * capacity, half_width
    )
    send_grads = fill_slots(out_grad[token_of], slot_ids, slot_count).reshape(
        ep_count, local_count * 2 * capacity, half_width
    )
    send_gates = fill_slots(route_gates.reshape(-1), own_slots, slot_count).reshape(
        ep_count, local_count * 2 * capacity
    )
    recv_rows, recv_grads, recv_gates = (
        lax.all_to_all(send_rows, "ep", split_axis=0, concat_axis=0, tiled=True),
        lax.all_to_all(send_grads, "ep", split_axis=0, concat_axis=0, tiled=True),
        lax.all_to_all(send_gates, "ep", split_axis=0, concat_axis=0, tiled=True),
    )
    shaped_rows = recv_rows.reshape(ep_count, local_count, 2, capacity, half_width)
    shaped_grads = recv_grads.reshape(ep_count, local_count, 2, capacity, half_width)
    shaped_gates = recv_gates.reshape(ep_count, local_count, 2, capacity)
    joined_rows, joined_grads = (
        lax.all_to_all(shaped_rows, "dp", split_axis=2, concat_axis=4, tiled=True),
        lax.all_to_all(shaped_grads, "dp", split_axis=2, concat_axis=4, tiled=True),
    )
    token_rows = joined_rows.reshape(ep_count, local_count, capacity, feature_width)
    grad_rows = joined_grads.reshape(ep_count, local_count, capacity, feature_width)
    gate_rows = lax.dynamic_index_in_dim(shaped_gates, lax.axis_index("dp"), 2, keepdims=False)
    row_grad, grad_gate_pre, grad_up_pre = expert_work(
        token_rows, grad_rows, gate_rows, w_gate, w_up, w_down
    )
    both_gate, both_up = share_pre_grads(
        grad_gate_pre.reshape(ep_count, local_count, 1, capacity, -1),
        grad_up_pre.reshape(ep_count, local_count, 1, capacity, -1),
    )
    spread = lax.all_to_all(
        row_grad.reshape(ep_count, local_count, 1, capacity, feature_width),
        "dp",
        split_axis=4,
        concat_axis=2,
        tiled=True,
    )
    grad_gate_w, grad_up_w = weight_terms(shaped_rows, both_gate, both_up)
    returned = lax.all_to_all(
        spread.reshape(ep_count, local_count * 2 * capacity, half_width),
        "ep",
        split_axis=0,
        concat_axis=0,
        tiled=True,
    )
    returned = returned.reshape(slot_count, half_width)
    per_route = (
        returned[slot_ids].astype(jnp.float32).reshape(2 * block_rows, top_count, half_width)
    )
    grad_input = jnp.sum(per_route, axis=1).astype(jnp.bfloat16)
    return (grad_input, grad_gate_w, grad_up_w)


ORDERS = ((0, 1, 2, 3), (1, 0, 2, 3), (2, 3, 1, 0), (3, 2, 1, 0))
LINES = len(ORDERS)
PARTS = 2
HALVES = 2
OUTER = ((0, 1), (1, 0), (2, 3), (3, 2))
INNER = ((1, 2), (2, 1))
TO_END = ((1, 0), (2, 3))
FROM_END = ((0, 1), (3, 2))


def along_line(value, moves):
    pairs = [(2 * a + side, 2 * b + side) for a, b in moves for side in range(2)]
    return lax.ppermute(value, "ep", pairs)


def across_pair(value):
    return lax.ppermute(value, "ep", [(i, i ^ 1) for i in range(2 * LINES)])


def across_cores(value):
    return lax.ppermute(value, "dp", [(0, 1), (1, 0)])


def tie(values, *others):
    values = list(values)
    return list(lax.optimization_barrier(tuple(values) + tuple(others))[: len(values)])


def gather_rows(rows, info, at_end, meanwhile):
    def widen(info, bits):
        came = [
            lax.ppermute(info, "ep", [(i, i ^ bit) for i in range(2 * LINES)]) for bit in bits
        ]
        return functools.reduce(jnp.add, came, info)

    outer, inner, other = along_line(rows, OUTER), along_line(rows, INNER), across_pair(rows)
    info = widen(info + across_cores(info), [1])
    info = widen(info, [2])
    outer, inner, other, info = tie((outer, inner, other, info))
    pieces = [rows, other]

    second, third = along_line(inner, TO_END), along_line(outer, INNER)
    other = across_pair(outer)
    info = widen(info, [4])
    second, third, other = tie((second, third, other))
    pieces += [outer, other]

    middle = jnp.where(at_end, second, inner)
    last, other = along_line(third, TO_END), across_pair(middle)
    done = meanwhile(0, info, pieces)
    last, other = tie((last, other), *done)
    pieces += [middle, other]

    meanwhile(1, info, [last, other])
    for part in range(2):
        far = jnp.where(at_end, last[part], third[part])
        pieces += [far, across_pair(far)]
        last, third = tie((last, third))
    return pieces


def scatter_sums(partial, meanwhile):
    f32, bf16 = jnp.float32, jnp.bfloat16

    def own_side(m, other):
        return partial[2 * m].astype(f32) + other.astype(f32)

    other = across_pair(partial[7])
    (other,) = meanwhile(0, [other])
    far = own_side(3, other)
    outward, other = along_line(far.astype(bf16), FROM_END), across_pair(partial[5])
    outward, other = meanwhile(1, [outward, other])
    middle = own_side(2, other)
    crossed = along_line((far + outward.astype(f32)).astype(bf16), INNER)
    outward, other = along_line(middle.astype(bf16), FROM_END), across_pair(partial[3])
    crossed, outward, other = meanwhile(2, [crossed, outward, other])
    near = own_side(1, other) + crossed.astype(f32)
    inner = along_line((middle + outward.astype(f32)).astype(bf16), INNER)
    outer, other = along_line(near.astype(bf16), OUTER), across_pair(partial[1])
    inner, outer, other = meanwhile(3, [inner, outer, other])
    total = own_side(0, other) + outer.astype(f32) + inner.astype(f32)
    return total.astype(bf16)


def route_kernel(order_ref, base_ref, info_ref, slot_ref, gate_ref, *, top_count, block_rows):
    local_count = slot_ref.shape[0]
    chunk = info_ref.shape[2]
    row = lax.broadcasted_iota(jnp.int32, (chunk, chunk), 0)
    column = lax.broadcasted_iota(jnp.int32, (chunk, chunk), 1)
    before = ((row < column) & (row // block_rows == column // block_rows)).astype(jnp.bfloat16)
    lane = lax.broadcasted_iota(jnp.int32, (local_count, chunk), 1)
    expert = (base_ref[0] + lax.broadcasted_iota(jnp.int32, (local_count, chunk), 0)).astype(
        jnp.float32
    )
    for piece in range(info_ref.shape[0]):
        info = info_ref[order_ref[piece]].astype(jnp.float32)
        named = jnp.zeros((local_count, chunk), jnp.float32)
        gate = jnp.zeros((local_count, chunk), jnp.float32)
        for k in range(top_count):
            match = info[k : k + 1, :] == expert
            named = jnp.where(match, 1.0, named)
            gate = jnp.where(match, info[top_count + k : top_count + k + 1, :], gate)
        rank = jnp.dot(
            named.astype(jnp.bfloat16), before, preferred_element_type=jnp.float32
        ).astype(jnp.int32)
        block = piece * (chunk // block_rows) + lane // block_rows
        columns = pl.ds(piece * chunk, chunk)
        slot_ref[:, columns] = jnp.where(named > 0.5, block * CAP + rank, -1)
        gate_ref[:, columns] = gate


def start_all(copies):
    for copy in copies:
        copy.start()
    return copies


def piece_copies(sources, rows_ref, sems):
    chunk = rows_ref.shape[0] // len(sources)
    return start_all(
        [
            pltpu.make_async_copy(source, rows_ref.at[pl.ds(m * chunk, chunk)], sems.at[m])
            for m, source in enumerate(sources)
        ]
    )


def group_copies(source, target, sems):
    count, number = target.shape[0], sems.shape[0]
    group = count // number
    return start_all(
        [
            pltpu.make_async_copy(
                source.at[pl.ds(i * group, group)], target.at[pl.ds(i * group, group)], sems.at[i]
            )
            for i in range(number)
        ]
    )


def hot_part(slot_ref, experts, part, slots):
    tokens = slot_ref.shape[1] // PARTS
    count = slots // PARTS
    columns = slice(part * tokens, (part + 1) * tokens)
    row = lax.broadcasted_iota(jnp.int32, (count, tokens), 0) + part * count
    return [row == slot_ref[e : e + 1, columns] for e in experts]


def dispatch(part, slot_ref, rows_ref, x_ref, start=0):
    local_count = x_ref.shape[0]
    count = 2 * LINES * 2 * CAP // PARTS
    first_slot = part * count if x_ref.shape[1] > count else 0
    group = min(8, local_count)
    for first in range(0, local_count, group):
        experts = range(start + first, start + first + group)
        hot = jnp.concatenate(
            [h.astype(jnp.bfloat16) for h in hot_part(slot_ref, experts, part, count * PARTS)]
        )
        found = jnp.dot(hot, rows_ref[...], preferred_element_type=jnp.float32)
        found = found.astype(jnp.bfloat16)
        for i, e in enumerate(experts):
            x_ref[e - start, first_slot : first_slot + count] = found[i * count : (i + 1) * count]


def first_kernel(slot_ref, gates_ref, *refs):
    pieces, (x_ref, grad_x_ref, slot_gates_ref) = refs[:4], refs[4:7]
    tokens_here, grads_here, token_sems, grad_sems = refs[7:]
    tokens = piece_copies([piece.at[0] for piece in pieces], tokens_here, token_sems)
    grads = piece_copies([piece.at[1] for piece in pieces], grads_here, grad_sems)
    for arrivals, rows_ref, target in (
        (tokens, tokens_here, x_ref),
        (grads, grads_here, grad_x_ref),
    ):
        for copy in arrivals:
            copy.wait()
        dispatch(0, slot_ref, rows_ref, target)
    local_count, slots, lanes = slot_gates_ref.shape
    tokens, count = slot_ref.shape[1] // PARTS, slots // PARTS
    for e in range(local_count):
        for part in range(PARTS):
            gates = gates_ref[e : e + 1, part * tokens : (part + 1) * tokens]
            gate = jnp.where(hot_part(slot_ref, [e], part, slots)[0], gates, 0.0)
            slot_gates_ref[e, part * count : (part + 1) * count] = jnp.broadcast_to(
                jnp.sum(gate, axis=1, keepdims=True), (count, lanes)
            )


def finish_slots(
    index, slot_ref, pieces, first_ref, rows_ref, x_here, piece_sems, first_sem, start=0
):
    sources = [piece.at[index] if len(piece.shape) == 3 else piece for piece in pieces]
    arrivals = piece_copies(sources, rows_ref, piece_sems)
    experts = pl.ds(start, x_here.shape[0])
    first = pltpu.make_async_copy(
        first_ref.at[experts], x_here.at[:, pl.ds(0, first_ref.shape[1])], first_sem
    )
    first.start()

    def finish():
        for copy in arrivals:
            copy.wait()
        dispatch(1, slot_ref, rows_ref, x_here, start)
        first.wait()

    return finish


def multiply(x_ref, w_ref, here, out_refs, out_sems, weights=None, side=0):
    groups = out_sems.shape[0]
    group = x_ref.shape[0] // groups
    copies = []
    for i in range(groups):
        if weights is not None:
            weights[i].wait()
        for e in range(i * group, (i + 1) * group):
            here[e] = lax.dot_general(
                x_ref[e],
                w_ref[e],
                (((1,), (side,)), ((), ())),
                preferred_element_type=jnp.float32,
            )
        span, each = pl.ds(i * group, group), groups // len(out_refs)
        target = out_refs[i // each].at[pl.ds(i % each * group, group)]
        copies += start_all([pltpu.make_async_copy(here.at[span], target, out_sems.at[i])])
    return copies


def load_kernel(w_ref, out_ref, sems):
    for copy in group_copies(w_ref, out_ref, sems):
        copy.wait()


def pre_kernel(slot_ref, *refs):
    pieces, refs = refs[:4], refs[4:]
    first_ref, gate_w, up_w, x_ref = refs[:4]
    gate_refs, up_refs = refs[4 : 4 + HALVES], refs[4 + HALVES : 4 + 2 * HALVES]
    refs = refs[4 + 2 * HALVES :]
    rows_here, x_here, up_w_here, gate_here, up_here = refs[:5]
    piece_sems, first_sem, up_w_sems, x_sem, gate_sems, up_sems = refs[5:]
    finish = finish_slots(
        0, slot_ref, pieces, first_ref, rows_here, x_here, piece_sems, first_sem
    )
    up_ws = group_copies(up_w, up_w_here, up_w_sems)
    finish()
    copies = start_all([pltpu.make_async_copy(x_here, x_ref, x_sem)])
    copies += multiply(x_here, gate_w, gate_here, gate_refs, gate_sems)
    copies += multiply(x_here, up_w_here, up_here, up_refs, up_sems, up_ws)
    for copy in copies:
        copy.wait()


def down_kernel(start, slot_ref, *refs):
    pieces, refs = refs[:4], refs[4:]
    first_ref, down_w, raw_ref = refs[:3]
    rows_here, x_here, w_here, here, piece_sems, first_sem, w_sems, out_sems = refs[3:]
    finish = finish_slots(
        1, slot_ref, pieces, first_ref, rows_here, x_here, piece_sems, first_sem, start
    )
    weights = group_copies(down_w.at[pl.ds(start, x_here.shape[0])], w_here, w_sems)
    finish()
    for copy in multiply(x_here, w_here, here, [raw_ref], out_sems, weights, 1):
        copy.wait()


def keep_row(row, e, rows_ref):
    count = row.shape[0] // PARTS
    for part in range(PARTS):
        rows_ref[part, e * count : (e + 1) * count] = row[part * count : (part + 1) * count]


def sum_rows(part, start, local_count, slot_ref, rows, slots):
    experts = range(start, start + local_count)
    hot = jnp.concatenate(
        [h.astype(jnp.bfloat16) for h in hot_part(slot_ref, experts, part, slots)]
    )
    return lax.dot_general(
        hot, rows, (((0,), (0,)), ((), ())), preferred_element_type=jnp.float32
    )


def give_out(total, outs_here, out_refs, out_sems):
    rows = total.shape[0] // len(out_refs)
    for i in range(len(out_refs)):
        outs_here[i] = total[i * rows : (i + 1) * rows].astype(jnp.bfloat16)
    return start_all(
        [
            pltpu.make_async_copy(outs_here.at[i], out_ref, out_sems.at[i])
            for i, out_ref in enumerate(out_refs)
        ]
    )


def rows_kernel(start, slot_ref, slot_gates_ref, *refs):
    sources, gate_w, up_w, refs = refs[:6], refs[6], refs[7], refs[8:]
    last = start > 0
    if last:
        before_ref, refs = refs[0], refs[1:]
    grads_ref, near_ref, refs = refs[0], refs[1], refs[2:]
    if last:
        out_refs, refs = refs[:LINES], refs[LINES:]
        outs_here, out_sems = refs[-2:]
    else:
        sum_ref, refs = refs[0], refs[1:]
    inputs_here, gate_here, up_here, grads_here, rows_ref = refs[:5]
    input_sems, gate_sems, up_sems, grads_sem, near_sem = refs[5:10]
    local_count, slots, hidden = inputs_here.shape[1:]
    groups = input_sems.shape[1]
    group = local_count // groups
    arrivals = []
    for i in range(groups):
        here, there = pl.ds(i * group, group), pl.ds(start + i * group, group)
        moves = [
            pltpu.make_async_copy(source.at[here], inputs_here.at[j, here], input_sems.at[j, i])
            for j, source in enumerate(sources)
        ]
        moves += [
            pltpu.make_async_copy(gate_w.at[there], gate_here.at[here], gate_sems.at[i]),
            pltpu.make_async_copy(up_w.at[there], up_here.at[here], up_sems.at[i]),
        ]
        arrivals.append(start_all(moves))
    for i in range(groups):
        for copy in arrivals[i]:
            copy.wait()
        for e in range(i * group, (i + 1) * group):
            pre_gate = inputs_here[0, e] + inputs_here[1, e]
            pre_up = inputs_here[2, e] + inputs_here[3, e]
            raw = inputs_here[4, e] + inputs_here[5, e]
            sigmoid = jax.nn.sigmoid(pre_gate)
            scaled = slot_gates_ref[start + e, :, :1] * raw * sigmoid
            grad_gate = (scaled * pre_up * (1.0 + pre_gate * (1.0 - sigmoid))).astype(jnp.bfloat16)
            grad_up = (scaled * pre_gate).astype(jnp.bfloat16)
            grads_here[e, :, :hidden] = grad_gate
            grads_here[e, :, hidden:] = grad_up
            turned = (((1,), (1,)), ((), ()))
            row = lax.dot_general(
                grad_gate, gate_here[e], turned, preferred_element_type=jnp.float32
            )
            row += lax.dot_general(grad_up, up_here[e], turned, preferred_element_type=jnp.float32)
            keep_row(row.astype(jnp.bfloat16), e, rows_ref)
    copies = start_all(
        [
            pltpu.make_async_copy(grads_here, grads_ref, grads_sem),
            pltpu.make_async_copy(rows_ref.at[0], near_ref, near_sem),
        ]
    )
    total = sum_rows(1, start, local_count, slot_ref, rows_ref[1], slots)
    if last:
        copies += give_out(total + before_ref[...], outs_here, out_refs, out_sems)
    else:
        sum_ref[...] = total
    for copy in copies:
        copy.wait()


def near_kernel(slot_ref, *refs):
    rows_refs, out_refs = refs[:HALVES], refs[HALVES : HALVES + LINES]
    rows_here, outs_here, row_sems, out_sems = refs[HALVES + LINES :]
    count = rows_here.shape[0] // HALVES
    copies = start_all(
        [
            pltpu.make_async_copy(ref, rows_here.at[pl.ds(i * count, count)], row_sems.at[i])
            for i, ref in enumerate(rows_refs)
        ]
    )
    for copy in copies:
        copy.wait()
    local_count = slot_ref.shape[0]
    slots = PARTS * rows_here.shape[0] // local_count
    total = sum_rows(0, 0, local_count, slot_ref, rows_here[...], slots)
    for copy in give_out(total, outs_here, out_refs, out_sems):
        copy.wait()


def weight_kernel(x_ref, grads_ref, *refs):
    gate_out_ref, up_out_ref = refs[-2:]
    hidden = gate_out_ref.shape[-1]
    for i in range(x_ref.shape[0]):
        found = lax.dot_general(
            x_ref[i], grads_ref[i], (((0,), (0,)), ((), ())), preferred_element_type=jnp.float32
        ).astype(jnp.bfloat16)
        gate_out_ref[i] = found[:, :hidden]
        up_out_ref[i] = found[:, hidden:]


def in_hbm(value):
    return pltpu.with_memory_space_constraint(value, pltpu.HBM)


def in_vmem(value):
    return pltpu.with_memory_space_constraint(value, pltpu.VMEM)


def params(mib):
    return pltpu.CompilerParams(vmem_limit_bytes=mib * 1024 * 1024)


def cost(flops, moved):
    return pl.CostEstimate(flops=int(flops), bytes_accessed=int(moved), transcendentals=0)


def gather_body(tokens, out_grad, route_gates, expert_ids, w_gate, w_up, w_down):
    ep_count = 2 * LINES
    local_count, half_width, hidden = w_gate.shape
    block_rows, top_count = expert_ids.shape
    chunk = 2 * block_rows
    token_count = ep_count * chunk
    slots = 2 * ep_count * CAP
    part_slots, part_tokens = slots // PARTS, token_count // PARTS
    place = lax.axis_index("ep")
    here, side = place // 2, place % 2
    at_end = (here == 0) | (here == LINES - 1)
    bf16, f32 = jnp.bfloat16, jnp.float32
    memory = pl.BlockSpec(memory_space=pl.ANY)
    smem = pl.BlockSpec(memory_space=pltpu.SMEM)
    vmem = pl.BlockSpec(memory_space=pltpu.VMEM)
    copies = pltpu.SemaphoreType.DMA

    own_info = jnp.concatenate([expert_ids.astype(bf16), route_gates], axis=1).T
    info = jnp.zeros((ep_count, 2 * top_count, chunk), bf16)
    info = lax.dynamic_update_slice(
        info, own_info[None], (place, 0, lax.axis_index("dp") * block_rows)
    )
    line_order = jnp.asarray(ORDERS, jnp.int32)[here]
    order = (2 * line_order[:, None] + jnp.stack([side, 1 - side])[None, :]).reshape(-1)

    weight_bytes = local_count * half_width * hidden * 2
    matmul_flops = 2 * local_count * slots * half_width * hidden
    hot_flops = local_count * slots * half_width * token_count
    groups = 4
    piece_sems, w_sems = copies((ep_count // PARTS,)), copies((groups,))
    rows_here = pltpu.VMEM((part_tokens, half_width), bf16)
    x_shape = jax.ShapeDtypeStruct((local_count, slots, half_width), bf16)
    x_here = pltpu.VMEM(x_shape.shape, bf16)
    w_here, down_here = pltpu.VMEM(w_gate.shape, bf16), pltpu.VMEM(w_down.shape, bf16)
    pre_shape = jax.ShapeDtypeStruct((local_count, slots, hidden), f32)
    half = local_count // HALVES
    part_of_pre = pltpu.HBM((half, slots, hidden), f32)
    pre_here = pltpu.VMEM(pre_shape.shape, f32)
    batch = 2 if local_count % 2 == 0 else 1

    def batched(*shape):
        return pl.BlockSpec((batch,) + shape, lambda e: (e, 0, 0))

    made = {}

    def beside_gather(turn, info, pieces):
        if turn == 1:
            (gate_w,) = tie([w_gate], *pieces)
            made["loaded"] = pl.pallas_call(
                load_kernel,
                out_shape=pltpu.VMEM(w_gate.shape, bf16),
                in_specs=[memory],
                out_specs=memory,
                scratch_shapes=[w_sems],
                compiler_params=params(24),
                cost_estimate=cost(0, weight_bytes),
                name="load",
            )(in_hbm(gate_w))
            return []
        made["slots"], made["gates"] = pl.pallas_call(
            functools.partial(route_kernel, top_count=top_count, block_rows=block_rows),
            out_shape=(
                jax.ShapeDtypeStruct((local_count, token_count), jnp.int32),
                jax.ShapeDtypeStruct((local_count, token_count), f32),
            ),
            in_specs=[smem, smem, vmem],
            out_specs=(vmem, vmem),
            compiler_params=params(16),
            cost_estimate=cost(1e7, 1e6),
            name="route",
        )(order, (place * local_count).reshape(1), info)
        part_shape = jax.ShapeDtypeStruct((local_count, part_slots, half_width), bf16)
        made["x"], made["grad_x"], made["slot_gates"] = pl.pallas_call(
            first_kernel,
            out_shape=(
                part_shape,
                part_shape,
                jax.ShapeDtypeStruct((local_count, slots, 128), f32),
            ),
            in_specs=[vmem] * 2 + [memory] * 4,
            out_specs=(vmem,) * 3,
            scratch_shapes=[rows_here, rows_here, piece_sems, piece_sems],
            compiler_params=params(32),
            cost_estimate=cost(hot_flops, weight_bytes / 2),
            name="first_slots",
        )(made["slots"], made["gates"], *pieces)
        return [made["x"], made["grad_x"]]

    pieces = gather_rows(jnp.stack([tokens, out_grad]), info, at_end, beside_gather)
    slot_of = made["slots"]

    x, *pre_parts = pl.pallas_call(
        pre_kernel,
        out_shape=(x_shape,) + (part_of_pre,) * (2 * HALVES),
        in_specs=[vmem] + [memory] * 5 + [vmem, memory],
        out_specs=(memory,) * (1 + 2 * HALVES),
        scratch_shapes=[rows_here, x_here, w_here, pre_here, pre_here]
        + [piece_sems, copies, w_sems, copies, w_sems, w_sems],
        compiler_params=params(24),
        cost_estimate=cost(hot_flops / 2 + 2 * matmul_flops, 2.8 * weight_bytes),
        name="pre",
    )(
        slot_of,
        *pieces[4:8],
        made["x"],
        in_vmem(made["loaded"]),
        in_hbm(w_up),
    )
    gate_parts, up_parts = pre_parts[:HALVES], pre_parts[HALVES:]
    grad_pieces = tie(pieces[8:], x)

    def down(start, pieces):
        return pl.pallas_call(
            functools.partial(down_kernel, start),
            out_shape=part_of_pre,
            in_specs=[vmem] + [memory] * 6,
            out_specs=memory,
            scratch_shapes=[
                rows_here,
                pltpu.VMEM((half, slots, half_width), bf16),
                pltpu.VMEM((half, hidden, half_width), bf16),
                pltpu.VMEM((half, slots, hidden), f32),
            ]
            + [piece_sems, copies, w_sems, w_sems],
            compiler_params=params(12),
            cost_estimate=cost((hot_flops / 2 + matmul_flops) / HALVES, 1.4 * weight_bytes / HALVES),
            name="down",
        )(slot_of, *pieces, made["grad_x"], in_hbm(w_down))

    piece_shape = jax.ShapeDtypeStruct((chunk, half_width), bf16)
    pieces_here = [pltpu.VMEM((LINES, chunk, half_width), bf16), copies((LINES,))]

    def rows(number, sources, before):
        scratch = [
            pltpu.VMEM((6, half, slots, hidden), f32),
            pltpu.VMEM((half, half_width, hidden), bf16),
            pltpu.VMEM((half, half_width, hidden), bf16),
            pltpu.VMEM((half, slots, 2 * hidden), bf16),
            pltpu.VMEM((PARTS, half * part_slots, half_width), bf16),
            copies((6, groups)),
            w_sems,
            w_sems,
            copies,
            copies,
        ]
        out_shape = [
            jax.ShapeDtypeStruct((half, slots, 2 * hidden), bf16),
            jax.ShapeDtypeStruct((half * part_slots, half_width), bf16),
        ]
        if before:
            out_shape += [piece_shape] * LINES
            out_specs = (memory,) * (2 + LINES)
            scratch += pieces_here
        else:
            out_shape += [pltpu.VMEM((part_tokens, half_width), f32)]
            out_specs = (memory, memory, vmem)
        return pl.pallas_call(
            functools.partial(rows_kernel, number * half),
            out_shape=tuple(out_shape),
            in_specs=[vmem] * 2 + [memory] * 8 + [vmem] * len(before),
            out_specs=out_specs,
            scratch_shapes=scratch,
            compiler_params=params(30),
            cost_estimate=cost(
                (2 * matmul_flops + hot_flops) / HALVES, 3.1 * weight_bytes / HALVES
            ),
            name="rows",
        )(slot_of, made["slot_gates"], *sources, in_hbm(w_gate), in_hbm(w_up), *before)

    def both(value):
        return [value, across_cores(value)]

    pre_first = [*both(gate_parts[0]), *both(up_parts[0])]
    raw_first = down(0, [*pieces[4:6], *grad_pieces])
    sent = both(raw_first)
    gate_last, up_last, *last_pieces = tie(
        [gate_parts[1], up_parts[1], *pieces[4:6], *grad_pieces], raw_first
    )
    pre_last = [*both(gate_last), *both(up_last)]
    raw_last = down(half, last_pieces)
    sent[1], pre_first[1], pre_first[3] = tie((sent[1], pre_first[1], pre_first[3]), raw_last)
    grads_first, near_first, sums = rows(0, [*pre_first, *sent], [])
    last = [*pre_last, *both(raw_last)]
    grads_last, near_last, *far_sums = rows(1, last, [in_vmem(sums)])
    grads = [grads_first, grads_last]
    near_first, near_last = tie((near_first, near_last), *far_sums)
    near_sums = pl.pallas_call(
        near_kernel,
        out_shape=(piece_shape,) * LINES,
        in_specs=[vmem] + [memory] * HALVES,
        out_specs=(memory,) * LINES,
        scratch_shapes=[
            pltpu.VMEM((local_count * part_slots, half_width), bf16),
            pieces_here[0],
            copies((HALVES,)),
            pieces_here[1],
        ],
        compiler_params=params(12),
        cost_estimate=cost(hot_flops / 2, weight_bytes / 3),
        name="near",
    )(slot_of, near_first, near_last)
    partial = [*near_sums, *far_sums]

    early, late = half * 5 // 8, half * 5 // 8
    spans = (
        ((0, early),),
        ((early, half), (half, local_count - 2 * (half - late))),
        ((local_count - 2 * (half - late), local_count - half + late),),
        ((local_count - half + late, local_count),),
    )
    weight_shape = jax.ShapeDtypeStruct(w_gate.shape, bf16)
    weight_grads = []

    def block_of(first, *shape):
        return pl.BlockSpec((1,) + shape, lambda e: (first + e, 0, 0))

    def meanwhile(turn, values):
        tied = held or partial
        for first, end in spans[turn]:
            operands = tie([x, grads[first // half]], *tied)
            weight_grads[:] = pl.pallas_call(
                weight_kernel,
                grid=(end - first,),
                out_shape=(weight_shape, weight_shape),
                in_specs=[block_of(first, slots, half_width), block_of(first % half, slots, 2 * hidden)]
                + [memory] * len(weight_grads),
                out_specs=(block_of(first, half_width, hidden), block_of(first, half_width, hidden)),
                input_output_aliases={2 + i: i for i in range(len(weight_grads))},
                compiler_params=params(32),
                cost_estimate=cost(
                    2 * matmul_flops * (end - first) / local_count,
                    2.5 * weight_bytes * (end - first) / local_count,
                ),
                name="weight_grads",
            )(*operands, *weight_grads)
        *values, weight_grads[0], weight_grads[1] = tie([*values, *weight_grads])
        held[:] = values
        return values

    held = []
    grad_input = scatter_sums(partial, meanwhile)
    return (grad_input, *weight_grads)


def solution(mesh):
    in_specs = (
        P(("groups", "ep"), "dp"),
        P(("groups", "ep"), "dp"),
        P(("groups", "ep", "dp"), None),
        P(("groups", "ep", "dp"), None),
        P("ep", "dp", None),
        P("ep", "dp", None),
        P("ep", None, "dp"),
    )
    out_specs = (
        P(("groups", "ep"), "dp"),
        P(("groups", "ep"), "dp", None),
        P(("groups", "ep"), "dp", None),
    )
    ep_count = mesh.shape["ep"]
    body = gather_body if ep_count == 2 * LINES else exchange_body
    return jax.shard_map(body, mesh=mesh, in_specs=in_specs, out_specs=out_specs, check_vma=False)
```
